32 devices in a mesh: dp: 4 (over y, x), ctx: 8 (over z, core).
Axes of the slice: x: 2, y: 2, z: 4, core: 2. Of those that a mesh axis runs over, the one named last changes fastest.
Arguments:
- tokens_in: bfloat16 [4, 1024, 2048], P('dp', 'ctx'), may hold values from -6 to 6
- exit_layer: int32 [4, 1024], P('dp', 'ctx'), may hold values from 8 to 23
- layer_index: int32 [1], replicated, may hold values from 8 to 15
- segment_ids: int32 [4, 1024], P('dp', 'ctx'), may hold values from 0 to 4, as said below
- grad_out: bfloat16 [4, 1024, 2048], P('dp', 'ctx'), may hold values from -6 to 6
- first_gain: bfloat16 [2048], P(('dp', 'ctx')), may hold values from 0.099609375 to 1.8984375
- first_bias: bfloat16 [2048], P(('dp', 'ctx')), may hold values from -1.75 to 1.75
- query_weight: bfloat16 [2048, 2048], P(('dp', 'ctx')), may hold values from -0.125 to 0.125
- query_bias: bfloat16 [2048], P(('dp', 'ctx')), may hold values from -1.75 to 1.75
- key_weight: bfloat16 [2048, 2048], P(('dp', 'ctx')), may hold values from -0.125 to 0.125
- value_weight: bfloat16 [2048, 2048], P(('dp', 'ctx')), may hold values from -0.125 to 0.125
- value_bias: bfloat16 [2048], P(('dp', 'ctx')), may hold values from -0.625 to 0.625
- out_weight: bfloat16 [2048, 2048], P(('dp', 'ctx')), may hold values from -1 to 1
- out_bias: bfloat16 [2048], P(('dp', 'ctx')), may hold values from -1.75 to 1.75
- second_gain: bfloat16 [2048], P(('dp', 'ctx')), may hold values from 0.099609375 to 1.8984375
- second_bias: bfloat16 [2048], P(('dp', 'ctx')), may hold values from -1.75 to 1.75
- up_weight: bfloat16 [2048, 8192], P(('dp', 'ctx')), may hold values from -0.125 to 0.125
- up_bias: bfloat16 [8192], P(('dp', 'ctx')), may hold values from -3 to 3
- down_weight: bfloat16 [8192, 2048], P(('dp', 'ctx')), may hold values from -0.0625 to 0.0625
- down_bias: bfloat16 [2048], P(('dp', 'ctx')), may hold values from -1.75 to 1.75
Outputs:
- layer_out: bfloat16 [4, 1024, 2048], P('dp', 'ctx')
- grad_in: bfloat16 [4, 1024, 2048], P('dp', 'ctx')
- grad_first_gain: float32 [2048], P(('dp', 'ctx'))
- grad_first_bias: float32 [2048], P(('dp', 'ctx'))
- grad_query_weight: float32 [2048, 2048], P(('dp', 'ctx'))
- grad_query_bias: float32 [2048], P(('dp', 'ctx'))
- grad_key_weight: float32 [2048, 2048], P(('dp', 'ctx'))
- grad_value_weight: float32 [2048, 2048], P(('dp', 'ctx'))
- grad_value_bias: float32 [2048], P(('dp', 'ctx'))
- grad_out_weight: float32 [2048, 2048], P(('dp', 'ctx'))
- grad_out_bias: float32 [2048], P(('dp', 'ctx'))
- grad_second_gain: float32 [2048], P(('dp', 'ctx'))
- grad_second_bias: float32 [2048], P(('dp', 'ctx'))
- grad_up_weight: float32 [2048, 8192], P(('dp', 'ctx'))
- grad_up_bias: float32 [8192], P(('dp', 'ctx'))
- grad_down_weight: float32 [8192, 2048], P(('dp', 'ctx'))
- grad_down_bias: float32 [2048], P(('dp', 'ctx'))
The draws below stay inside these ranges and needn't reach their ends.
Inputs may be any that keep to these rules, and one draw needn't show every extreme that they name: `segment_ids`: in each row the ids start at 0, never fall and rise by one at four places, so a row holds five segments; segment 2 begins within the row's first 128 positions and ends within its last 128; the other four are each shorter than 128.
All inputs are finite; a program needn't handle non-finite values.
Results may differ from the reference program's by a relative error of at most 0.015.
Values may be sent and summed in bfloat16 or wider, within the bound.
No kernel may reach another device: no remote copies, remote signals or barrier semaphores. Data moves between devices by JAX's collectives and lax.ppermute only.
A program may use at most 512 MiB of HBM per device.

```python
import jax
import jax.numpy as jnp
from jax import lax

D = 2048
HEADS = 32
HEAD_DIM = 64
FF = 8192
POS_DEV = 128
SEQ = 1024
ROWS = 4


def draw_segment_ids(key, part):
    key = jax.random.fold_in(key, 11)
    keys = jax.random.split(key, 4)
    first_cut = jax.random.randint(keys[0], (ROWS, 1), 2, POS_DEV)
    extra_front = 1 + jax.random.randint(keys[1], (ROWS, 1), 0, POS_DEV) % (first_cut - 1)
    last_cut = jax.random.randint(keys[2], (ROWS, 1), SEQ - POS_DEV + 1, SEQ - 1)
    extra_back = last_cut + 1 + jax.random.randint(keys[3], (ROWS, 1), 0, SEQ) % (SEQ - last_cut - 1)
    position = jnp.arange(SEQ, dtype=jnp.int32)[None, :]
    ids = (position >= extra_front).astype(jnp.int32) + (position >= first_cut).astype(jnp.int32)
    ids = ids + (position >= last_cut).astype(jnp.int32) + (position >= extra_back).astype(jnp.int32)
    return ids.astype(jnp.int32)


def touch_ends(drawn, stream_key, smallest, largest):
    spot = [jax.random.randint(jax.random.fold_in(stream_key, axis), (), 0, length) for axis, length in enumerate(drawn.shape)]
    widest = drawn.shape.index(max(drawn.shape))
    beside = spot[:widest] + [(spot[widest] + 1) % drawn.shape[widest]] + spot[widest + 1:]
    return drawn.at[tuple(spot)].set(smallest).at[tuple(beside)].set(largest)


def strengthened(drawn, stream_key, source, target, shards_of, factor):
    owner, partner = [(jnp.arange(drawn.shape[dim]) // (drawn.shape[dim] // shards_of)).reshape([-1 if axis == dim else 1 for axis in range(drawn.ndim)]) for dim in (source, target)]
    chosen = jax.random.permutation(stream_key, shards_of)[partner]
    strong = (owner == chosen) | (owner == (partner + shards_of // 2) % shards_of)
    return jnp.where(strong, factor * drawn, drawn)


def block_scale(own_key, shape, cuts, least, high):
    factor_of, own = 1.0, jax.random.fold_in(own_key, 6)
    for dim, blocks in cuts:
        heights = jnp.exp(jax.random.uniform(jax.random.fold_in(own, dim), (blocks,), jnp.float32, least / len(cuts), high / len(cuts)))
        factor_of = factor_of * jnp.repeat(heights, shape[dim] // blocks).reshape([-1 if axis == dim else 1 for axis in range(len(shape))])
    return factor_of


def bell_draw(key, shape, spread, most, cuts=(), held_as=jnp.bfloat16):
    loudness = block_scale(key, shape, cuts, -0.22, 0.18) if cuts else 1.0
    values = jax.random.normal(key, shape, jnp.float32) * spread * loudness
    return jnp.minimum(jnp.maximum(values, -most), most).astype(held_as)


def bell_draw_with(own_key, extent, spread, most, pieces, heavy, held_as=jnp.bfloat16):
    array = spread * jax.random.normal(own_key, extent, jnp.float32)
    if pieces:
        array = array * block_scale(own_key, extent, pieces, -0.22, 0.18)
    return jnp.clip(strengthened(array, jax.random.fold_in(own_key, 3), *heavy), -most, most).astype(held_as)


def setup_inputs(seed: int = 0) -> dict:
    splits = jax.random.split(jax.random.key(seed), 21)
    tokens_in = bell_draw(splits[0], (ROWS, SEQ, D), 1.0, 6.0, ((0, 4), (1, 8)))
    exit_layer = touch_ends(jax.random.randint(splits[1], (ROWS, SEQ), 8, 24), jax.random.fold_in(splits[1], 1), 8, 23).astype(jnp.int32)
    layer_index = jax.random.randint(splits[2], (1,), 8, 16).astype(jnp.int32)
    segment_ids = draw_segment_ids(jax.random.fold_in(splits[20], 71), 0)
    grad_out = bell_draw_with(splits[4], (ROWS, SEQ, D), 1.0, 6.0, ((0, 4), (1, 8)), (1, 2, 8, 2.0))
    first_gain = jnp.clip(1.0 + 0.18 * jax.random.normal(splits[5], (D,), jnp.float32), 0.099609375, 1.8984375).astype(jnp.bfloat16)
    first_bias = bell_draw(splits[6], (D,), 0.3, 1.75, ((0, 32),))
    query_weight = bell_draw(splits[7], (D, D), D ** -0.5, 0.125, ((0, 32),))
    query_bias = bell_draw(splits[8], (D,), 0.3, 1.75, ((0, 32),))
    key_weight = bell_draw(splits[9], (D, D), D ** -0.5, 0.125, ((0, 32),))
    value_weight = bell_draw(splits[10], (D, D), D ** -0.5, 0.125, ((0, 32),))
    value_bias = bell_draw(splits[11], (D,), 0.1, 0.625, ((0, 32),))
    out_weight = bell_draw(splits[12], (D, D), (D // 64) ** -0.5, 1.0, ((0, 32),))
    out_bias = bell_draw(splits[13], (D,), 0.3, 1.75, ((0, 32),))
    second_gain = jnp.clip(1.0 + 0.18 * jax.random.normal(splits[14], (D,), jnp.float32), 0.099609375, 1.8984375).astype(jnp.bfloat16)
    second_bias = bell_draw(splits[15], (D,), 0.3, 1.75, ((0, 32),))
    up_weight = bell_draw(splits[16], (D, FF), D ** -0.5, 0.125, ((0, 32),))
    up_bias = bell_draw(splits[17], (FF,), 0.5, 3.0, ((0, 32),))
    down_weight = bell_draw(splits[18], (FF, D), FF ** -0.5, 0.0625, ((0, 32),))
    down_bias = bell_draw(splits[19], (D,), 0.3, 1.75, ((0, 32),))
    return dict(tokens_in=tokens_in, exit_layer=exit_layer, layer_index=layer_index, segment_ids=segment_ids, grad_out=grad_out, first_gain=first_gain, first_bias=first_bias, query_weight=query_weight, query_bias=query_bias, key_weight=key_weight, value_weight=value_weight, value_bias=value_bias, out_weight=out_weight, out_bias=out_bias, second_gain=second_gain, second_bias=second_bias, up_weight=up_weight, up_bias=up_bias, down_weight=down_weight, down_bias=down_bias)


EPSILON = 1e-05
NEG_FILL = -1e+30

@jax.custom_vjp
def low(v):
    return lax.optimization_barrier(v.astype(jnp.bfloat16)).astype(jnp.float32)

@jax.custom_vjp
def low_back(v):
    return v

def low_keep(v):
    return (low(v), None)

def low_pass(kept, grad):
    return (grad,)

def back_keep(v):
    return (v, None)

def back_low(kept, grad):
    return (low(grad),)
low.defvjp(low_keep, low_pass)
low_back.defvjp(back_keep, back_low)

def matmul(left, right):
    return jnp.dot(left, right, precision=lax.Precision.HIGHEST)

def normalize(values_in, gain_vec, bias_vec):
    average = lax.optimization_barrier(jnp.mean(values_in, axis=-1, keepdims=True))
    centered = values_in - average
    variance = lax.optimization_barrier(jnp.mean(centered * centered, axis=-1, keepdims=True))
    return centered * lax.rsqrt(variance + EPSILON) * gain_vec + bias_vec

def attention(queries, keys, values, row_segs):
    scale = HEAD_DIM ** (-0.5)
    block = 512 if SEQ % 512 == 0 else SEQ
    count = SEQ // block
    positions = jnp.arange(SEQ, dtype=jnp.int32)

    def one_block(item):
        query_block, pos_block, seg_block = item
        raw = jnp.einsum('qhd,khd->hqk', query_block, keys, precision=lax.Precision.HIGHEST)
        scores = low_back(raw * scale)
        allowed = (seg_block[:, None] == row_segs[None, :]) & (positions[None, :] <= pos_block[:, None])
        scores = jnp.where(allowed[None], scores, NEG_FILL)
        top = lax.optimization_barrier(jnp.max(scores, axis=-1, keepdims=True))
        log_total = top + jnp.log(lax.optimization_barrier(jnp.sum(jnp.exp(scores - top), axis=-1, keepdims=True)))
        probs = jnp.exp(scores - log_total)
        return jnp.einsum('hqk,khd->qhd', low(probs), values, precision=lax.Precision.HIGHEST)
    blocks = lax.map(jax.checkpoint(one_block), (queries.reshape(count, block, HEADS, HEAD_DIM), positions.reshape(count, block), row_segs.reshape(count, block)))
    return blocks.reshape(SEQ, HEADS * HEAD_DIM)

def row_forward(params, row_in, row_active, row_segs):
    first_gain, first_bias, query_weight, query_bias, key_weight, value_weight, value_bias, out_weight, out_bias, second_gain, second_bias, up_weight, up_bias, down_weight, down_bias = params
    head_shape = (SEQ, HEADS, HEAD_DIM)
    normed_one = low(normalize(row_in, first_gain, first_bias))
    queries = low(low_back(matmul(normed_one, query_weight) + query_bias))
    keys = low(low_back(matmul(normed_one, key_weight)))
    values = low(low_back(matmul(normed_one, value_weight) + value_bias))
    heads = attention(queries.reshape(head_shape), keys.reshape(head_shape), values.reshape(head_shape), row_segs)
    mixed = low(low_back(heads))
    branch = low_back(matmul(mixed, out_weight) + out_bias)
    middle = row_in + row_active[:, None] * branch
    normed_two = low(normalize(middle, second_gain, second_bias))
    hidden = low(jax.nn.gelu(low_back(matmul(normed_two, up_weight) + up_bias), approximate=True))
    feed = low_back(matmul(hidden, down_weight) + down_bias)
    return middle + row_active[:, None] * feed

def reference(tokens_in, exit_layer, layer_index, segment_ids, grad_out, first_gain, first_bias, query_weight, query_bias, key_weight, value_weight, value_bias, out_weight, out_bias, second_gain, second_bias, up_weight, up_bias, down_weight, down_bias):
    params = tuple((item.astype(jnp.float32) for item in (first_gain, first_bias, query_weight, query_bias, key_weight, value_weight, value_bias, out_weight, out_bias, second_gain, second_bias, up_weight, up_bias, down_weight, down_bias)))
    active = (exit_layer > layer_index[0]).astype(jnp.float32)

    def one_row(totals, row):
        row_in, row_active, row_segs, row_grad = row

        def forward_fn(weights, inputs):
            return row_forward(weights, inputs, row_active, row_segs)
        result, pullback = jax.vjp(forward_fn, params, row_in.astype(jnp.float32))
        grad_params, grad_row = pullback(row_grad.astype(jnp.float32))
        totals = jax.tree.map(lambda first, second: first + second, totals, grad_params)
        return (totals, (result.astype(jnp.bfloat16), grad_row.astype(jnp.bfloat16)))
    zeros = jax.tree.map(jnp.zeros_like, params)
    totals, outputs = lax.scan(one_row, zeros, (tokens_in, active, segment_ids, grad_out))
    layer_out, grad_in = outputs
    return (layer_out, grad_in, totals[0], totals[1], totals[2], totals[3], totals[4], totals[5], totals[6], totals[7], totals[8], totals[9], totals[10], totals[11], totals[12], totals[13], totals[14])
```

```python
import jax
import jax.numpy as jnp
from jax import lax
from jax.experimental import pallas as pl
from jax.experimental.pallas import tpu as pltpu
from jax.sharding import PartitionSpec as P

HEADS = 32
HEAD_DIM = 64
EPSILON = 1e-05
NEG_FILL = -1e30
SCALE = HEAD_DIM ** (-0.5)
QUERY_BLOCK = 256
BF16 = jnp.bfloat16
F32 = jnp.float32

NN = (((1,), (0,)), ((), ()))
NT = (((1,), (1,)), ((), ()))
TN = (((0,), (0,)), ((), ()))


def dot(left, right, dims=NN):
    return lax.dot_general(left, right, dims, preferred_element_type=F32)


def forward_kernel(qkv_ref, seg_col_ref, seg_row_ref, mixed_ref, log_ref, *, heads, lanes, block):
    rows = qkv_ref.shape[0]
    head_of_lane = lax.broadcasted_iota(jnp.int32, (1, lanes), 1) // HEAD_DIM
    diagonal = lax.broadcasted_iota(jnp.int32, (block, block), 1) <= lax.broadcasted_iota(
        jnp.int32, (block, block), 0
    )
    for b in range(rows // block):
        low, high = b * block, (b + 1) * block
        queries = qkv_ref[low:high, :lanes] * jnp.asarray(SCALE, BF16)
        keys = qkv_ref[:high, lanes : 2 * lanes]
        values = qkv_ref[:high, 2 * lanes :]
        allowed = seg_col_ref[low:high, :] == seg_row_ref[:, :high]
        last = allowed[:, low:] & diagonal
        allowed = jnp.concatenate([allowed[:, :low], last], axis=1) if b else last
        mixed = jnp.zeros((block, lanes), F32)
        for h in range(heads):
            mine = head_of_lane == h
            scores = dot(jnp.where(mine, queries, jnp.zeros_like(queries)), keys, NT)
            scores = jnp.where(allowed, scores, NEG_FILL)
            top = jnp.max(scores, axis=1, keepdims=True)
            weights = jnp.exp(scores - top)
            total = jnp.sum(weights, axis=1, keepdims=True)
            product = dot(weights.astype(BF16), values)
            mixed = mixed + jnp.where(mine, product / total, 0.0)
            log_total = jnp.broadcast_to(top + jnp.log(total), (block, 128))
            log_ref[h : h + 1, low:high] = jnp.transpose(log_total)[:1, :]
        mixed_ref[low:high, :] = mixed.astype(BF16)


def backward_kernel(
    qkv_ref, grad_ref, log_ref, delta_ref, seg_col_ref, seg_row_ref, out_ref, dk_ref, dv_ref, *, heads, lanes, block
):
    rows = qkv_ref.shape[0]
    head_of_lane = lax.broadcasted_iota(jnp.int32, (1, lanes), 1) // HEAD_DIM
    diagonal = lax.broadcasted_iota(jnp.int32, (block, block), 0) <= lax.broadcasted_iota(
        jnp.int32, (block, block), 1
    )
    scale = jnp.asarray(SCALE, BF16)
    for b in range(rows // block):
        low, high = b * block, (b + 1) * block
        queries = qkv_ref[low:high, :lanes] * scale
        grads = grad_ref[low:high, :]
        keys = qkv_ref[:high, lanes : 2 * lanes]
        values = qkv_ref[:high, 2 * lanes :]
        allowed = seg_col_ref[:high, :] == seg_row_ref[:, low:high]
        last = allowed[low:, :] & diagonal
        allowed = jnp.concatenate([allowed[:low, :], last], axis=0) if b else last
        grad_queries = jnp.zeros((block, lanes), F32)
        grad_keys = jnp.zeros((high, lanes), F32)
        grad_values = jnp.zeros((high, lanes), F32)
        for h in range(heads):
            mine = head_of_lane == h
            query_h = jnp.where(mine, queries, jnp.zeros_like(queries))
            grad_h = jnp.where(mine, grads, jnp.zeros_like(grads))
            scores = dot(keys, query_h, NT)
            probs = jnp.where(allowed, jnp.exp(scores - log_ref[h : h + 1, low:high]), 0.0)
            grad_probs = dot(values, grad_h, NT)
            grad_scores = (probs * (grad_probs - delta_ref[h : h + 1, low:high])).astype(BF16)
            grad_values = grad_values + dot(probs.astype(BF16), grad_h)
            grad_keys = grad_keys + dot(grad_scores, query_h)
            grad_queries = grad_queries + jnp.where(mine, dot(grad_scores, keys, TN), 0.0)
        out_ref[low:high, :lanes] = (grad_queries * SCALE).astype(BF16)
        if b:
            dk_ref[:low, :] = dk_ref[:low, :] + grad_keys[:low, :]
            dv_ref[:low, :] = dv_ref[:low, :] + grad_values[:low, :]
        dk_ref[low:high, :] = grad_keys[low:, :]
        dv_ref[low:high, :] = grad_values[low:, :]
    out_ref[:, lanes : 2 * lanes] = dk_ref[...].astype(BF16)
    out_ref[:, 2 * lanes :] = dv_ref[...].astype(BF16)


def attention_forward(qkv, seg_col, seg_row):
    rows, lanes = qkv.shape[0], qkv.shape[1] // 3
    heads = lanes // HEAD_DIM
    pairs = rows * rows * heads // 2
    return pl.pallas_call(
        lambda *refs: forward_kernel(*refs, heads=heads, lanes=lanes, block=QUERY_BLOCK),
        out_shape=(jax.ShapeDtypeStruct((rows, lanes), BF16), jax.ShapeDtypeStruct((heads, rows), F32)),
        compiler_params=pltpu.CompilerParams(vmem_limit_bytes=48 * 2**20),
        cost_estimate=pl.CostEstimate(flops=pairs * 1024, bytes_accessed=8 * rows * lanes, transcendentals=pairs),
        name="attention_forward",
    )(qkv, seg_col, seg_row)


def attention_backward(qkv, grads, log_total, delta, seg_col, seg_row):
    rows, lanes = qkv.shape[0], qkv.shape[1] // 3
    heads = lanes // HEAD_DIM
    pairs = rows * rows * heads // 2
    return pl.pallas_call(
        lambda *refs: backward_kernel(*refs, heads=heads, lanes=lanes, block=QUERY_BLOCK),
        out_shape=jax.ShapeDtypeStruct((rows, 3 * lanes), BF16),
        scratch_shapes=[pltpu.VMEM((rows, lanes), F32), pltpu.VMEM((rows, lanes), F32)],
        compiler_params=pltpu.CompilerParams(vmem_limit_bytes=48 * 2**20),
        cost_estimate=pl.CostEstimate(flops=pairs * 2560, bytes_accessed=14 * rows * lanes, transcendentals=pairs),
        name="attention_backward",
    )(qkv, grads, log_total, delta, seg_col, seg_row)


def chips():
    return lax.axis_size("ctx") // 2


def turn(value, k):
    count = chips()
    return lax.ppermute(
        value, "ctx", [(2 * s + core, 2 * ((s + k) % count) + core) for s in range(count) for core in range(2)]
    )


def swap(value):
    return lax.ppermute(value, "ctx", [(i, i ^ 1) for i in range(2 * chips())])


def place():
    me = lax.axis_index("ctx")
    return me // 2, me % 2


def gather_ctx(block):
    count = chips()
    chip, core = place()
    same = [block] + [turn(block, k) for k in range(1, count)]
    other = [swap(item) for item in same]
    out = jnp.zeros((2 * count,) + block.shape, block.dtype)
    for k in range(count):
        base = 2 * ((chip + count - k) % count)
        out = lax.dynamic_update_index_in_dim(out, same[k], base + core, 0)
        out = lax.dynamic_update_index_in_dim(out, other[k], base + 1 - core, 0)
    return out


def exchange_ctx(blocks):
    count = chips()
    chip, core = place()
    pairs = blocks.reshape((count, 2) + blocks.shape[1:])
    same = []
    for k in range(count):
        piece = lax.dynamic_index_in_dim(pairs, (chip + k) % count, 0, keepdims=False)
        same.append(turn(piece, k) if k else piece)
    mine = [lax.dynamic_index_in_dim(item, core, 0, keepdims=False) for item in same]
    other = swap(jnp.stack([lax.dynamic_index_in_dim(item, 1 - core, 0, keepdims=False) for item in same]))
    out = jnp.zeros(blocks.shape, blocks.dtype)
    for k in range(count):
        base = 2 * ((chip + count - k) % count)
        out = lax.dynamic_update_index_in_dim(out, mine[k], base + core, 0)
        out = lax.dynamic_update_index_in_dim(out, other[k], base + 1 - core, 0)
    return out


def split_rows(rows):
    count = chips()
    chip, core = place()
    pairs = rows.reshape((count, 2, rows.shape[0] // (2 * count), rows.shape[1]))
    turned = [lax.dynamic_index_in_dim(pairs, (chip + k) % count, 0, keepdims=False) for k in range(1, count + 1)]
    pick = lambda which: jnp.concatenate(
        [lax.dynamic_index_in_dim(item, which, 0, keepdims=False) for item in turned], axis=0
    )
    return pick(core), pick(1 - core)


def reduce_ctx(left, right, dims):
    count = chips()
    mine, other = split_rows(left)
    arrived = swap(dot(other, right, dims).astype(BF16))
    own = dot(mine, right, dims)
    n = own.shape[0] // count
    sums = [own[k * n : (k + 1) * n] + arrived[k * n : (k + 1) * n].astype(F32) for k in range(count)]
    total = sums[-1]
    for k in range(1, count):
        total = total + turn(sums[k - 1].astype(BF16), k).astype(F32)
    return total


def reduce_ctx_small(blocks):
    count = chips()
    chip, core = place()
    pairs = blocks.reshape(count, 2, blocks.shape[1])
    arrived = swap(lax.dynamic_index_in_dim(pairs, 1 - core, 1, keepdims=False))
    sums = arrived + lax.dynamic_index_in_dim(pairs, core, 1, keepdims=False)
    total = lax.dynamic_index_in_dim(sums, chip, 0, keepdims=False)
    for k in range(1, count):
        total = total + turn(lax.dynamic_index_in_dim(sums, (chip + k) % count, 0, keepdims=False), k)
    return total


def gather_dp_small(value):
    parts = lax.axis_size("dp")
    me = lax.axis_index("dp")
    out = jnp.zeros((parts,) + value.shape, value.dtype)
    out = lax.dynamic_update_index_in_dim(out, value, me, 0)
    for k in range(1, parts):
        arrived = lax.ppermute(value, "dp", [(i, (i + k) % parts) for i in range(parts)])
        out = lax.dynamic_update_index_in_dim(out, arrived, (me + parts - k) % parts, 0)
    return out


def reduce_dp_small(blocks):
    parts = lax.axis_size("dp")
    me = lax.axis_index("dp")
    total = lax.dynamic_index_in_dim(blocks, me, 0, keepdims=False)
    for k in range(1, parts):
        piece = lax.dynamic_index_in_dim(blocks, (me + k) % parts, 0, keepdims=False)
        total = total + lax.ppermute(piece, "dp", [(i, (i + k) % parts) for i in range(parts)])
    return total


def gather_dp(value):
    return lax.all_gather(value, "dp", axis=0, tiled=True)


def scatter_dp(value):
    return lax.psum_scatter(value, "dp", scatter_dimension=0, tiled=True)


def standardize(values):
    average = jnp.mean(values, axis=-1, keepdims=True)
    centered = values - average
    variance = jnp.mean(centered * centered, axis=-1, keepdims=True)
    factor = lax.rsqrt(variance + EPSILON)
    return centered * factor, factor


def norm_back(grad, gain, standard, factor):
    scaled = grad * gain
    return (
        scaled
        - jnp.mean(scaled, axis=-1, keepdims=True)
        - standard * jnp.mean(scaled * standard, axis=-1, keepdims=True)
    ) * factor


def smooth(pre_act):
    return jax.nn.gelu(pre_act, approximate=True)


def smooth_slope(u):
    inner = 0.7978845608028654 * (u + 0.044715 * u * u * u)
    bend = jnp.tanh(inner)
    return 0.5 * (1.0 + bend) + 0.5 * u * (1.0 - bend * bend) * 0.7978845608028654 * (1.0 + 3.0 * 0.044715 * u * u)


def local(
    tokens_in,
    exit_layer,
    layer_index,
    segment_ids,
    grad_out,
    first_gain,
    first_bias,
    query_weight,
    query_bias,
    key_weight,
    value_weight,
    value_bias,
    out_weight,
    out_bias,
    second_gain,
    second_bias,
    up_weight,
    up_bias,
    down_weight,
    down_bias,
):
    T, N = lax.axis_size("ctx"), lax.axis_size("dp")
    me = lax.axis_index("ctx")
    n, D = tokens_in.shape[1], tokens_in.shape[2]
    r = first_gain.shape[0]
    f = up_bias.shape[0]
    S = T * n
    B = max(HEAD_DIM, r)
    A = D // (T * B)
    L = A * B
    x = tokens_in[0]
    g_out = grad_out[0]
    active = (exit_layer[0] > layer_index[0]).astype(F32)

    def columns(weight, lead, width):
        return weight.reshape(r, lead, T, width).transpose(2, 0, 1, 3).reshape(T, r, lead * width)

    qkv_send = jnp.concatenate([columns(w, A, B) for w in (query_weight, key_weight, value_weight)], axis=2)
    w_qkv = gather_dp(exchange_ctx(qkv_send).reshape(T * r, 3 * L))
    natural = r % HEAD_DIM == 0
    if natural:
        w_out = gather_dp(out_weight)
    else:
        w_all = lax.all_gather(out_weight, ("dp", "ctx"), axis=0, tiled=True).reshape(A, T, B, D)
        w_out = lax.dynamic_index_in_dim(w_all, me, 1, keepdims=False).reshape(L, D)
    w_up = gather_dp(exchange_ctx(columns(up_weight, N, f)).reshape(T * r, N * f))
    w_down = gather_dp(down_weight)

    small = jnp.concatenate(
        [first_gain, first_bias, query_bias, value_bias, out_bias, second_gain, second_bias, down_bias, up_bias]
    )
    small_dp = gather_dp_small(small).reshape(-1)
    flags = jnp.concatenate([active.astype(BF16), segment_ids[0].astype(BF16)])
    small_all = gather_ctx(jnp.concatenate([small_dp, flags]))
    params = small_all[:, : N * (8 * r + f)].reshape(T, N, 8 * r + f).transpose(1, 0, 2)
    feature = lambda i: params[:, :, i * r : (i + 1) * r].reshape(D).astype(F32)
    gain_one, bias_one, bias_query, bias_value, bias_out, gain_two, bias_two, bias_down = (
        feature(i) for i in range(8)
    )
    bias_up = lax.dynamic_index_in_dim(params, me, 1, keepdims=False)[:, 8 * r :].reshape(N * f).astype(F32)
    active_row = small_all[:, -2 * n : -n].reshape(S)
    segs = small_all[:, -n:].reshape(S).astype(jnp.int32)
    seg_col, seg_row = segs.reshape(S, 1), segs.reshape(1, S)
    own_heads = lambda v: lax.dynamic_index_in_dim(v.reshape(A, T, B), me, 1, keepdims=False).reshape(L)
    bias_qkv = jnp.concatenate([own_heads(bias_query), jnp.zeros((L,), F32), own_heads(bias_value)])

    x_all = gather_ctx(x).reshape(S, D)
    standard_one, _ = standardize(x_all.astype(F32))
    normed_one = (standard_one * gain_one + bias_one).astype(BF16)
    qkv = (dot(normed_one, w_qkv) + bias_qkv).astype(BF16)
    mixed, log_total = attention_forward(qkv, seg_col, seg_row)
    branch = reduce_ctx(mixed, w_out, NN) + bias_out
    inputs = x.astype(F32)
    active_own = active[:, None]
    middle = inputs + active_own * branch

    standard_two, factor_two = standardize(middle)
    normed_two = (standard_two * gain_two + bias_two).astype(BF16)
    g_all = gather_ctx(g_out).reshape(S, D)
    normed_two_all = gather_ctx(normed_two).reshape(S, D)
    pre_act = dot(normed_two_all, w_up) + bias_up
    hidden = smooth(pre_act).astype(BF16)
    feed = reduce_ctx(hidden, w_down, NN)
    layer_out = (middle + active_own * (feed + bias_down)).astype(BF16)[None]

    grad_ffn = (active_row[:, None] * g_all).astype(BF16)
    grad_hidden = dot(grad_ffn, w_down, NT)
    grad_pre = (grad_hidden * smooth_slope(pre_act)).astype(BF16)
    grad_normed_two = reduce_ctx(grad_pre, w_up, NT)
    grad_down = scatter_dp(dot(hidden, grad_ffn, TN).astype(BF16)).astype(F32)
    grad_up_mine = scatter_dp(dot(normed_two_all, grad_pre, TN).astype(BF16))

    def rows_back(mine, lead, width):
        got = exchange_ctx(mine.reshape(T, r, lead * width))
        return got.reshape(T, r, lead, width).transpose(1, 2, 0, 3).reshape(r, lead * T * width).astype(F32)

    grad_up = rows_back(grad_up_mine, N, f)
    grad_res = g_out.astype(F32)
    grad_middle = grad_res + norm_back(grad_normed_two, gain_two, standard_two, factor_two)
    grad_branch = (active_own * grad_middle).astype(BF16)

    grad_branch_all = gather_ctx(grad_branch).reshape(S, D)
    grad_heads = dot(grad_branch_all, w_out, NT).astype(BF16)
    delta = jnp.sum(
        (grad_heads.astype(F32) * mixed.astype(F32)).reshape(S, L // HEAD_DIM, HEAD_DIM), axis=2
    ).transpose()
    grad_qkv = attention_backward(qkv, grad_heads, log_total, delta, seg_col, seg_row)
    grad_normed_one = reduce_ctx(grad_qkv, w_qkv, NT)
    grad_out_w = dot(mixed, grad_branch_all, TN)
    if natural:
        grad_out_w = scatter_dp(grad_out_w.astype(BF16)).astype(F32)
    else:
        spread = jnp.zeros((A, T, B, D), F32)
        spread = lax.dynamic_update_index_in_dim(spread, grad_out_w.reshape(A, B, D), me, 1)
        grad_out_w = lax.psum_scatter(spread.reshape(D, D), ("dp", "ctx"), scatter_dimension=0, tiled=True)
    grad_qkv_mine = scatter_dp(dot(normed_one, grad_qkv, TN).astype(BF16))
    got = exchange_ctx(grad_qkv_mine.reshape(T, r, 3 * L)).reshape(T, r, 3, A, B)
    grad_q, grad_k, grad_v = (
        got[:, :, i].transpose(1, 2, 0, 3).reshape(r, D).astype(F32) for i in range(3)
    )
    standard_in, factor_in = standardize(inputs)
    grad_in = (grad_middle + norm_back(grad_normed_one, gain_one, standard_in, factor_in)).astype(BF16)[None]

    partial_one = dot(grad_qkv, w_qkv, NT)
    grad_gain_one = jnp.sum(partial_one * standard_one, axis=0)
    grad_bias_one = jnp.sum(partial_one, axis=0)
    grad_gain_two = jnp.sum(grad_normed_two * standard_two, axis=0)
    grad_bias_two = jnp.sum(grad_normed_two, axis=0)
    ctx_index = lax.broadcasted_iota(jnp.int32, (1, T, 1), 1)
    spread_heads = lambda v: jnp.where(ctx_index == me, v.reshape(A, 1, B), 0.0).reshape(D)
    grad_bias_qkv = jnp.sum(grad_qkv.astype(F32), axis=0)
    grad_out_sum = jnp.sum(grad_branch.astype(F32), axis=0)
    grad_down_sum = jnp.sum((active_own * grad_res), axis=0)
    grad_up_sum = jnp.sum(grad_pre.astype(F32), axis=0)
    features = jnp.stack(
        [
            grad_gain_one,
            grad_bias_one,
            spread_heads(grad_bias_qkv[:L]),
            spread_heads(grad_bias_qkv[2 * L :]),
            grad_out_sum,
            grad_gain_two,
            grad_bias_two,
            grad_down_sum,
        ]
    )
    features = features.reshape(8, N, T, r).transpose(2, 1, 0, 3).reshape(T, N, 8 * r)
    units = jnp.where(
        lax.broadcasted_iota(jnp.int32, (T, 1, 1), 0) == me, grad_up_sum.reshape(1, N, f), 0.0
    )
    sums = jnp.concatenate([features, units], axis=2).reshape(T, N * (8 * r + f))
    sums = reduce_dp_small(reduce_ctx_small(sums).reshape(N, 8 * r + f))
    shard = lambda i: sums[i * r : (i + 1) * r]
    return (
        layer_out,
        grad_in,
        shard(0),
        shard(1),
        grad_q,
        shard(2),
        grad_k,
        grad_v,
        shard(3),
        grad_out_w,
        shard(4),
        shard(5),
        shard(6),
        grad_up,
        sums[8 * r :],
        grad_down,
        shard(7),
    )


def solution(mesh):
    rows = P("dp", "ctx", None)
    flags = P("dp", "ctx")
    vector = P(("dp", "ctx"))
    matrix = P(("dp", "ctx"), None)
    in_specs = (
        rows, flags, P(), flags, rows, vector, vector, matrix, vector, matrix,
        matrix, vector, matrix, vector, vector, vector, matrix, vector, matrix, vector,
    )
    out_specs = (
        rows, rows, vector, vector, matrix, vector, matrix, matrix, vector, matrix,
        vector, vector, vector, matrix, vector, matrix, vector,
    )
    return jax.shard_map(local, mesh=mesh, in_specs=in_specs, out_specs=out_specs, check_vma=False)
```

```python
import jax
import jax.numpy as jnp
from jax import lax
from jax.experimental import pallas as pl
from jax.experimental.pallas import tpu as pltpu
from jax.sharding import PartitionSpec as P

HEADS = 32
HEAD_DIM = 64
EPSILON = 1e-05
NEG_FILL = -1e30
SCALE = HEAD_DIM ** (-0.5)
QUERY_BLOCK = 256
BF16 = jnp.bfloat16
F32 = jnp.float32

NN = (((1,), (0,)), ((), ()))
NT = (((1,), (1,)), ((), ()))
TN = (((0,), (0,)), ((), ()))
ANYWHERE = pl.BlockSpec(memory_space=pl.ANY)


def dot(left, right, dims=NN):
    return lax.dot_general(left, right, dims, preferred_element_type=F32)


def forward_kernel(*refs, heads, lanes, block):
    qkv_ref, seg_col_ref, seg_row_ref = refs[:3]
    mixed_ref, log_ref = refs[-2:]
    rows = qkv_ref.shape[0]
    head_of_lane = lax.broadcasted_iota(jnp.int32, (1, lanes), 1) // HEAD_DIM
    diagonal = lax.broadcasted_iota(jnp.int32, (block, block), 1) <= lax.broadcasted_iota(
        jnp.int32, (block, block), 0
    )
    for b in range(rows // block):
        low, high = b * block, (b + 1) * block
        queries = qkv_ref[low:high, :lanes] * jnp.asarray(SCALE, BF16)
        keys = qkv_ref[:high, lanes : 2 * lanes]
        values = qkv_ref[:high, 2 * lanes :]
        allowed = seg_col_ref[low:high, :] == seg_row_ref[:, :high]
        last = allowed[:, low:] & diagonal
        allowed = jnp.concatenate([allowed[:, :low], last], axis=1) if b else last
        mixed = jnp.zeros((block, lanes), F32)
        for h in range(heads):
            mine = head_of_lane == h
            scores = dot(jnp.where(mine, queries, jnp.zeros_like(queries)), keys, NT)
            scores = jnp.where(allowed, scores, NEG_FILL)
            top = jnp.max(scores, axis=1, keepdims=True)
            weights = jnp.exp(scores - top)
            total = jnp.sum(weights, axis=1, keepdims=True)
            product = dot(weights.astype(BF16), values)
            mixed = mixed + jnp.where(mine, product / total, 0.0)
            log_total = jnp.broadcast_to(top + jnp.log(total), (block, 128))
            log_ref[h : h + 1, low:high] = jnp.transpose(log_total)[:1, :]
        mixed_ref[low:high, :] = mixed.astype(BF16)


def backward_kernel(*refs, heads, lanes, block):
    qkv_ref, grad_ref, log_ref, mixed_ref, seg_col_ref, seg_row_ref = refs[:6]
    out_ref, dk_ref, dv_ref = refs[-3:]
    rows = qkv_ref.shape[0]
    head_of_lane = lax.broadcasted_iota(jnp.int32, (1, lanes), 1) // HEAD_DIM
    diagonal = lax.broadcasted_iota(jnp.int32, (block, block), 0) <= lax.broadcasted_iota(
        jnp.int32, (block, block), 1
    )
    scale = jnp.asarray(SCALE, BF16)
    head_rows = jnp.where(lax.broadcasted_iota(jnp.int32, (16, lanes), 0) == head_of_lane, 1.0, 0.0).astype(BF16)
    for b in range(rows // block):
        low, high = b * block, (b + 1) * block
        queries = qkv_ref[low:high, :lanes] * scale
        grads = grad_ref[low:high, :]
        keys = qkv_ref[:high, lanes : 2 * lanes]
        values = qkv_ref[:high, 2 * lanes :]
        allowed = seg_col_ref[:high, :] == seg_row_ref[:, low:high]
        last = allowed[low:, :] & diagonal
        allowed = jnp.concatenate([allowed[:low, :], last], axis=0) if b else last
        products = grads.astype(F32) * mixed_ref[low:high, :].astype(F32)
        coarse = products.astype(BF16)
        fine = (products - coarse.astype(F32)).astype(BF16)
        delta = dot(head_rows, coarse, NT) + dot(head_rows, fine, NT)
        grad_queries = jnp.zeros((block, lanes), F32)
        grad_keys = jnp.zeros((high, lanes), F32)
        grad_values = jnp.zeros((high, lanes), F32)
        for h in range(heads):
            mine = head_of_lane == h
            query_h = jnp.where(mine, queries, jnp.zeros_like(queries))
            grad_h = jnp.where(mine, grads, jnp.zeros_like(grads))
            scores = dot(keys, query_h, NT)
            probs = jnp.where(allowed, jnp.exp(scores - log_ref[h : h + 1, low:high]), 0.0)
            grad_probs = dot(values, grad_h, NT)
            grad_scores = (probs * (grad_probs - delta[h : h + 1, :])).astype(BF16)
            grad_values = grad_values + dot(probs.astype(BF16), grad_h)
            grad_keys = grad_keys + dot(grad_scores, query_h)
            grad_queries = grad_queries + jnp.where(mine, dot(grad_scores, keys, TN), 0.0)
        out_ref[low:high, :lanes] = (grad_queries * SCALE).astype(BF16)
        if b:
            dk_ref[:low, :] = dk_ref[:low, :] + grad_keys[:low, :]
            dv_ref[:low, :] = dv_ref[:low, :] + grad_values[:low, :]
        dk_ref[low:high, :] = grad_keys[low:, :]
        dv_ref[low:high, :] = grad_values[low:, :]
    out_ref[:, lanes : 2 * lanes] = dk_ref[...].astype(BF16)
    out_ref[:, 2 * lanes :] = dv_ref[...].astype(BF16)


def attention_forward(qkv, seg_col, seg_row, earlier):
    rows, lanes = qkv.shape[0], qkv.shape[1] // 3
    heads = lanes // HEAD_DIM
    pairs = rows * rows * heads // 2
    return pl.pallas_call(
        lambda *refs: forward_kernel(*refs, heads=heads, lanes=lanes, block=QUERY_BLOCK),
        out_shape=(jax.ShapeDtypeStruct((rows, lanes), BF16), jax.ShapeDtypeStruct((heads, rows), F32)),
        compiler_params=pltpu.CompilerParams(vmem_limit_bytes=48 * 2**20),
        cost_estimate=pl.CostEstimate(flops=pairs * 5000, bytes_accessed=8 * rows * lanes, transcendentals=pairs),
        in_specs=[pl.BlockSpec(memory_space=pltpu.VMEM)] * 3 + [ANYWHERE] * len(earlier),
        name="attention_forward",
    )(qkv, seg_col, seg_row, *earlier)


def attention_backward(qkv, grads, log_total, mixed, seg_col, seg_row, earlier):
    rows, lanes = qkv.shape[0], qkv.shape[1] // 3
    heads = lanes // HEAD_DIM
    pairs = rows * rows * heads // 2
    return pl.pallas_call(
        lambda *refs: backward_kernel(*refs, heads=heads, lanes=lanes, block=QUERY_BLOCK),
        out_shape=jax.ShapeDtypeStruct((rows, 3 * lanes), BF16),
        scratch_shapes=[pltpu.VMEM((rows, lanes), F32), pltpu.VMEM((rows, lanes), F32)],
        compiler_params=pltpu.CompilerParams(vmem_limit_bytes=48 * 2**20),
        cost_estimate=pl.CostEstimate(flops=pairs * 5000, bytes_accessed=14 * rows * lanes, transcendentals=pairs),
        in_specs=[pl.BlockSpec(memory_space=pltpu.VMEM)] * 6 + [ANYWHERE] * len(earlier),
        name="attention_backward",
    )(qkv, grads, log_total, mixed, seg_col, seg_row, *earlier)


def chips():
    return lax.axis_size("ctx") // 2


def turn(value, k):
    count = chips()
    return lax.ppermute(
        value, "ctx", [(2 * s + core, 2 * ((s + k) % count) + core) for s in range(count) for core in range(2)]
    )


def swap(value):
    return lax.ppermute(value, "ctx", [(i, i ^ 1) for i in range(2 * chips())])


def place():
    me = lax.axis_index("ctx")
    return me // 2, me % 2


def after(value, *earlier, cost=0):
    def nothing(*refs):
        pass

    return pl.pallas_call(
        nothing,
        out_shape=jax.ShapeDtypeStruct(value.shape, value.dtype),
        in_specs=[ANYWHERE] * (1 + len(earlier)),
        out_specs=ANYWHERE,
        input_output_aliases={0: 0},
        cost_estimate=pl.CostEstimate(flops=cost * 10**9, bytes_accessed=cost * 3 * 10**6, transcendentals=0),
        name="after",
    )(value, *earlier)


def gather_ctx(block):
    count = chips()
    chip, core = place()
    same = [block] + [turn(block, k) for k in range(1, count)]
    chip_of = [(chip + count - k) % count for k in range(count)]
    other = [swap(item) for item in same]
    out = jnp.zeros((2 * count,) + block.shape, block.dtype)
    for k in range(count):
        base = 2 * chip_of[k]
        out = lax.dynamic_update_index_in_dim(out, same[k], base + core, 0)
        out = lax.dynamic_update_index_in_dim(out, other[k], base + 1 - core, 0)
    return out, same[1]


def where_am_i():
    return jnp.stack(place()).astype(jnp.int32)


def pack_columns(weights, cuts, vectors):
    count = chips()
    r = weights[0].shape[0]
    total = sum(lead * width for lead, width in cuts)
    below = -(-len(vectors) // 16) * 16

    def kernel(at_ref, *refs):
        ins, outs = refs[: len(weights)], refs[-(count + 1) :]
        chip, core = at_ref[0], at_ref[1]
        for j in range(2 * count):
            pieces = [
                ref[:, (a * 2 * count + j) * width : (a * 2 * count + j + 1) * width]
                for ref, (lead, width) in zip(ins, cuts)
                for a in range(lead)
            ]
            block = jnp.concatenate(pieces, axis=1)
            slot = lax.rem(j // 2 + count - chip, count)
            for k in range(count):

                @pl.when((slot == k) & (core == j % 2))
                def _(k=k, block=block):
                    outs[k][:r, :] = block

                @pl.when((slot == k) & (core != j % 2))
                def _(k=k, block=block):
                    outs[count][k, :r, :] = block

        if vectors:
            lines = [ref[...].astype(F32) for ref in refs[len(weights) : len(weights) + len(vectors)]]
            lines = [
                jnp.concatenate([line, jnp.zeros((1, total - line.shape[1]), F32)], axis=1) for line in lines
            ]
            more = jnp.concatenate(lines + [jnp.zeros((below - len(lines), total), F32)], axis=0).astype(BF16)
            for k in range(count):
                outs[k][r:, :] = more
                outs[count][k, r:, :] = more

    block_shape = jax.ShapeDtypeStruct((r + below, total), BF16)
    return pl.pallas_call(
        kernel,
        out_shape=[block_shape] * count + [jax.ShapeDtypeStruct((count,) + block_shape.shape, BF16)],
        in_specs=[pl.BlockSpec(memory_space=pltpu.SMEM)]
        + [pl.BlockSpec(memory_space=pltpu.VMEM)] * (len(weights) + len(vectors)),
        name="pack_columns",
    )(where_am_i(), *weights, *vectors)


def pack_rows(arrays, more, height):
    count = chips()
    width = sum(item.shape[1] for item in arrays)
    below = more.shape[1]

    def kernel(at_ref, *refs):
        ins, outs = refs[: len(arrays)], refs[-(count + 1) :]
        chip, core = at_ref[0], at_ref[1]
        for k in range(count):
            base = 2 * lax.rem(chip + k, count)
            start = 0
            for ref in ins:
                end = start + ref.shape[1]
                mine = pl.ds(pl.multiple_of((base + core) * height, height), height)
                other = pl.ds(pl.multiple_of((base + 1 - core) * height, height), height)
                outs[k][:height, start:end] = ref[mine, :]
                outs[count][k, :height, start:end] = ref[other, :]
                start = end
            outs[k][height:, :] = refs[len(arrays)][base + core]
            outs[count][k, height:, :] = refs[len(arrays)][base + 1 - core]

    block_shape = jax.ShapeDtypeStruct((height + below, width), BF16)
    return pl.pallas_call(
        kernel,
        out_shape=[block_shape] * count + [jax.ShapeDtypeStruct((count,) + block_shape.shape, BF16)],
        in_specs=[pl.BlockSpec(memory_space=pltpu.SMEM)] + [pl.BlockSpec(memory_space=pltpu.VMEM)] * (1 + len(arrays)),
        name="pack_rows",
    )(where_am_i(), *arrays, more)


def exchange_ctx(packed):
    count = chips()
    arrived = swap(packed[count])
    both = [jnp.stack([packed[k], arrived[k]]) for k in range(count)]
    return [both[0]] + [turn(both[k], k) for k in range(1, count)]


def source_index(at_ref, k, side, count):
    core = at_ref[1] if side == 0 else 1 - at_ref[1]
    return 2 * lax.rem(at_ref[0] + count - k, count) + core


def unpack_to_rows(got, r, widths, earlier):
    count = chips()
    height, total = got[0].shape[1:]
    below = height - r

    def kernel(at_ref, *refs):
        ins, outs = refs[:count], refs[count + len(earlier) :]
        for k in range(count):
            for side in range(2):
                index = source_index(at_ref, k, side, count)
                start = 0
                for out, width in zip(outs, widths):
                    out[pl.ds(pl.multiple_of(index * r, r), r), :] = ins[k][side, :r, start : start + width]
                    start += width
                if below:
                    outs[-1][index] = ins[k][side, r:, :]

    return pl.pallas_call(
        kernel,
        out_shape=[jax.ShapeDtypeStruct((2 * count * r, width), BF16) for width in widths]
        + [jax.ShapeDtypeStruct((2 * count, below, total), BF16)] * (below > 0),
        in_specs=[pl.BlockSpec(memory_space=pltpu.SMEM)]
        + [pl.BlockSpec(memory_space=pltpu.VMEM)] * count
        + [ANYWHERE] * len(earlier),
        name="unpack_to_rows",
    )(where_am_i(), *got, *earlier)


def unpack_to_columns(got, r, cuts):
    count = chips()
    height, total = got[0].shape[1:]

    def kernel(at_ref, *refs):
        ins, outs, held = refs[:count], refs[count:-1], refs[-1]
        for k in range(count):
            for side in range(2):
                held[source_index(at_ref, k, side, count)] = ins[k][side]
        for j in range(2 * count):
            block = held[j, :r, :].astype(F32)
            start = 0
            for out, (lead, width) in zip(outs, cuts):
                for a in range(lead):
                    column = (a * 2 * count + j) * width
                    out[:, column : column + width] = block[:, start : start + width]
                    start += width
        below = held[0, r:, :].astype(F32)
        for j in range(1, 2 * count):
            below = below + held[j, r:, :].astype(F32)
        outs[-1][...] = jnp.sum(below, axis=0, keepdims=True)

    return pl.pallas_call(
        kernel,
        out_shape=[jax.ShapeDtypeStruct((r, 2 * count * lead * width), F32) for lead, width in cuts]
        + [jax.ShapeDtypeStruct((1, total), F32)],
        in_specs=[pl.BlockSpec(memory_space=pltpu.SMEM)] + [pl.BlockSpec(memory_space=pltpu.VMEM)] * count,
        scratch_shapes=[pltpu.VMEM((2 * count, height, total), BF16)],
        name="unpack_to_columns",
    )(where_am_i(), *got)


def split_rows(rows):
    count = chips()
    chip, core = place()
    pairs = rows.reshape((count, 2, rows.shape[0] // (2 * count), rows.shape[1]))
    order = [(chip + k) % count for k in range(1, count + 1)]
    turned = [lax.dynamic_index_in_dim(pairs, index, 0, keepdims=False) for index in order]
    pick = lambda which: jnp.concatenate(
        [lax.dynamic_index_in_dim(item, which, 0, keepdims=False) for item in turned], axis=0
    )
    return pick(core), pick(1 - core)


def chip_sums(left, right, dims, earlier=()):
    count = chips()
    mine, other = split_rows(left)
    leaving = dot(other, right, dims).astype(BF16)
    arrived = swap(after(leaving, *earlier) if earlier else leaving)
    own = dot(mine, right, dims)
    n = own.shape[0] // count
    sums = [own[k * n : (k + 1) * n] + arrived[k * n : (k + 1) * n].astype(F32) for k in range(count)]
    return [item.astype(BF16) for item in sums[:-1]] + sums[-1:]


def add_over_chips(sums, earlier=()):
    count = chips()
    total = sums[-1]
    for k in range(1, count):
        arrived = turn(sums[k - 1], k)
        arrived = after(arrived, *earlier) if earlier else arrived
        total = total + arrived.astype(F32)
        first = arrived if k == 1 else first
    return total, first


def reduce_dp_small(blocks):
    parts = lax.axis_size("dp")
    me = lax.axis_index("dp")
    total = lax.dynamic_index_in_dim(blocks, me, 0, keepdims=False)
    for k in range(1, parts):
        piece = lax.dynamic_index_in_dim(blocks, (me + k) % parts, 0, keepdims=False)
        total = total + lax.ppermute(piece, "dp", [(i, (i + k) % parts) for i in range(parts)])
    return total


def gather_dp(value):
    return lax.all_gather(value, "dp", axis=0, tiled=True)


def scatter_dp(value):
    return lax.psum_scatter(value, "dp", scatter_dimension=0, tiled=True)


def across(value, k):
    return lax.ppermute(value, "dp", [(i, i ^ k) for i in range(lax.axis_size("dp"))])


def turn_gather_dp(value):
    parts = lax.axis_size("dp")
    me = lax.axis_index("dp")
    out = jnp.zeros((parts,) + value.shape, value.dtype)
    out = lax.dynamic_update_index_in_dim(out, value, me, 0)
    for k in range(1, parts):
        out = lax.dynamic_update_index_in_dim(out, across(value, k), me ^ k, 0)
    return out.reshape((parts * value.shape[0],) + value.shape[1:])


def turn_scatter_dp(blocks):
    parts = lax.axis_size("dp")
    me = lax.axis_index("dp")
    blocks = blocks.reshape((parts, blocks.shape[0] // parts) + blocks.shape[1:])
    total = lax.dynamic_index_in_dim(blocks, me, 0, keepdims=False).astype(F32)
    for k in range(1, parts):
        total = total + across(lax.dynamic_index_in_dim(blocks, me ^ k, 0, keepdims=False), k).astype(F32)
    return total


def standardize(values):
    average = jnp.mean(values, axis=-1, keepdims=True)
    centered = values - average
    variance = jnp.mean(centered * centered, axis=-1, keepdims=True)
    factor = lax.rsqrt(variance + EPSILON)
    return centered * factor, factor


def norm_back(grad, gain, standard, factor):
    scaled = grad * gain
    return (
        scaled
        - jnp.mean(scaled, axis=-1, keepdims=True)
        - standard * jnp.mean(scaled * standard, axis=-1, keepdims=True)
    ) * factor


def smooth(pre_act):
    return jax.nn.gelu(pre_act, approximate=True)


def smooth_slope(u):
    inner = 0.7978845608028654 * (u + 0.044715 * u * u * u)
    bend = jnp.tanh(inner)
    return 0.5 * (1.0 + bend) + 0.5 * u * (1.0 - bend * bend) * 0.7978845608028654 * (1.0 + 3.0 * 0.044715 * u * u)


def local(
    tokens_in,
    exit_layer,
    layer_index,
    segment_ids,
    grad_out,
    first_gain,
    first_bias,
    query_weight,
    query_bias,
    key_weight,
    value_weight,
    value_bias,
    out_weight,
    out_bias,
    second_gain,
    second_bias,
    up_weight,
    up_bias,
    down_weight,
    down_bias,
):
    T, N = lax.axis_size("ctx"), lax.axis_size("dp")
    me = lax.axis_index("ctx")
    n, D = tokens_in.shape[1], tokens_in.shape[2]
    r = first_gain.shape[0]
    f = up_bias.shape[0]
    S = T * n
    B = max(HEAD_DIM, r)
    A = D // (T * B)
    L = A * B
    x = tokens_in[0]
    g_out = grad_out[0]
    active = (exit_layer[0] > layer_index[0]).astype(F32)

    x_all = lax.all_gather(x, "ctx", axis=0, tiled=True)
    natural = r % HEAD_DIM == 0
    if natural:
        w_out = turn_gather_dp(out_weight)
    else:
        w_all = lax.all_gather(out_weight, ("dp", "ctx"), axis=0, tiled=True).reshape(A, T, B, D)
        w_out = lax.dynamic_index_in_dim(w_all, me, 1, keepdims=False).reshape(L, D)
    vectors = [first_gain, first_bias, query_bias, value_bias, out_bias, second_gain, second_bias, down_bias, up_bias]
    vectors = [v.reshape(1, -1) for v in vectors + [active.astype(BF16), segment_ids[0].astype(BF16)]]
    got = exchange_ctx(pack_columns([query_weight, key_weight, value_weight], [(A, B)] * 3, vectors))
    qkv_rows, small_got = unpack_to_rows(got, r, (3 * L,), (x_all, w_out))
    up_packed = pack_columns([up_weight], [(N, f)], [])
    w_qkv = gather_dp(qkv_rows)
    small_width = max(r, f)
    params = turn_gather_dp(small_got[:, :9, :small_width].reshape(T * 9, small_width)).reshape(N, T, 9, small_width)
    g_all, g_begun = gather_ctx(after(g_out, qkv_rows))
    g_all = g_all.reshape(S, D)

    feature = lambda i: params[:, :, i, :r].reshape(D).astype(F32)
    gain_one, bias_one, bias_query, bias_value, bias_out, gain_two, bias_two, bias_down = (
        feature(i) for i in range(8)
    )
    bias_up = lax.dynamic_index_in_dim(params[:, :, 8, :f], me, 1, keepdims=False).reshape(N * f).astype(F32)
    active_row = small_got[:, 9, :n].reshape(S)
    segs = small_got[:, 10, :n].reshape(S).astype(jnp.int32)
    seg_col, seg_row = segs.reshape(S, 1), segs.reshape(1, S)
    own_heads = lambda v: lax.dynamic_index_in_dim(v.reshape(A, T, B), me, 1, keepdims=False).reshape(L)
    bias_qkv = jnp.concatenate([own_heads(bias_query), jnp.zeros((L,), F32), own_heads(bias_value)])

    standard_one, _ = standardize(x_all.astype(F32))
    normed_one = after((standard_one * gain_one + bias_one).astype(BF16), g_all)
    qkv = (dot(normed_one, w_qkv) + bias_qkv).astype(BF16)
    w_down = gather_dp(after(down_weight, qkv))
    up_got = exchange_ctx([*up_packed[:-1], after(up_packed[-1], g_begun)])
    mixed, log_total = attention_forward(qkv, seg_col, seg_row, ())
    (up_rows,) = unpack_to_rows(up_got, r, (N * f,), (mixed,))
    w_up = gather_dp(up_rows)
    branch = add_over_chips(chip_sums(mixed, w_out, NN, (up_rows,)))[0] + bias_out
    inputs = x.astype(F32)
    active_own = active[:, None]
    middle = inputs + active_own * branch

    standard_two, factor_two = standardize(middle)
    normed_two = (standard_two * gain_two + bias_two).astype(BF16)
    normed_two_all = gather_ctx(after(normed_two, cost=0))[0].reshape(S, D)
    pre_act = dot(normed_two_all, w_up) + bias_up
    hidden = smooth(pre_act).astype(BF16)

    grad_ffn = (active_row[:, None] * g_all).astype(BF16)
    grad_hidden = dot(grad_ffn, w_down, NT)
    grad_pre = (grad_hidden * smooth_slope(pre_act)).astype(BF16)
    sums_two = chip_sums(grad_pre, w_up, NT)
    grad_normed_two, begun_two = add_over_chips(sums_two)
    hidden = after(hidden, sums_two[0])
    grad_down_part = dot(hidden, grad_ffn, TN).astype(BF16)
    grad_down = scatter_dp(grad_down_part)
    grad_up_part = dot(after(normed_two_all, sums_two[0]), grad_pre, TN).astype(BF16)
    grad_up_mine = scatter_dp(grad_up_part)
    feed_sums = chip_sums(after(hidden, begun_two), w_down, NN)
    grad_res = g_out.astype(F32)
    grad_middle = grad_res + norm_back(grad_normed_two, gain_two, standard_two, factor_two)
    grad_branch = after((active_own * grad_middle).astype(BF16), cost=250)

    grad_branch_all = gather_ctx(grad_branch)[0].reshape(S, D)
    grad_heads = dot(grad_branch_all, w_out, NT).astype(BF16)
    grad_out_w = dot(mixed, grad_branch_all, TN)
    if natural:
        grad_out_w = scatter_dp(grad_out_w.astype(BF16))
    else:
        spread = jnp.zeros((A, T, B, D), F32)
        spread = lax.dynamic_update_index_in_dim(spread, grad_out_w.reshape(A, B, D), me, 1)
        grad_out_w = lax.psum_scatter(spread.reshape(D, D), ("dp", "ctx"), scatter_dimension=0, tiled=True)
    grad_qkv = attention_backward(
        qkv, grad_heads, log_total, mixed, seg_col, seg_row, (grad_down, grad_up_mine)
    )

    grad_qkv_part = dot(normed_one, grad_qkv, TN).astype(BF16)
    feed, _ = add_over_chips([after(item, grad_branch_all) for item in feed_sums[:-1]] + feed_sums[-1:], (grad_qkv,))
    sums_one = chip_sums(grad_qkv, w_qkv, NT, (grad_qkv_part, feed, grad_out_w))
    grad_normed_one, _ = add_over_chips(sums_one)
    grad_normed_one = after(grad_normed_one, cost=0)
    layer_out = (middle + active_own * (feed + bias_down)).astype(BF16)[None]
    standard_in, factor_in = standardize(inputs)
    grad_in = (grad_middle + norm_back(grad_normed_one, gain_one, standard_in, factor_in)).astype(BF16)[None]

    grad_gain_one = jnp.sum(grad_normed_one * standard_in, axis=0)
    grad_bias_one = jnp.sum(grad_normed_one, axis=0)
    grad_gain_two = jnp.sum(grad_normed_two * standard_two, axis=0)
    grad_bias_two = jnp.sum(grad_normed_two, axis=0)
    ctx_index = lax.broadcasted_iota(jnp.int32, (1, T, 1), 1)
    spread_heads = lambda v: jnp.where(ctx_index == me, v.reshape(A, 1, B), 0.0).reshape(D)
    grad_bias_qkv = jnp.sum(grad_qkv.astype(F32), axis=0)
    grad_out_sum = jnp.sum(grad_branch.astype(F32), axis=0)
    grad_down_sum = jnp.sum((active_own * grad_res), axis=0)
    grad_up_sum = jnp.sum(grad_pre.astype(F32), axis=0)
    features = jnp.stack(
        [
            grad_gain_one,
            grad_bias_one,
            spread_heads(grad_bias_qkv[:L]),
            spread_heads(grad_bias_qkv[2 * L :]),
            grad_out_sum,
            grad_gain_two,
            grad_bias_two,
            grad_down_sum,
        ]
    )
    features = features.reshape(8, N, T, r).transpose(1, 2, 0, 3).reshape(N, T, 8 * r)
    units = jnp.where(
        lax.broadcasted_iota(jnp.int32, (1, T, 1), 1) == me, grad_up_sum.reshape(N, 1, f), 0.0
    )
    sums = jnp.concatenate([features, units], axis=2).reshape(N, T * (8 * r + f))
    sums = reduce_dp_small(sums).reshape(T, 8 * r + f)
    grad_qkv_mine = scatter_dp(grad_qkv_part)
    coarse = sums.astype(BF16)
    fine = (sums - coarse.astype(F32)).astype(BF16)
    more = jnp.stack([coarse, fine], axis=1)
    more = jnp.pad(more, ((0, 0), (0, 14), (0, 3 * L + N * f - more.shape[2])))
    grad_got = exchange_ctx(pack_rows([after(grad_qkv_mine, grad_normed_one), grad_up_mine], more, r))
    grad_q, grad_k, grad_v, grad_up, sums = unpack_to_columns(grad_got, r, [(A, B)] * 3 + [(N, f)])
    sums = sums[0, : 8 * r + f]
    begun_one = grad_got[0]
    shard = lambda i: sums[i * r : (i + 1) * r]
    return (
        layer_out,
        grad_in,
        shard(0),
        shard(1),
        grad_q,
        shard(2),
        grad_k,
        grad_v,
        shard(3),
        grad_out_w.astype(F32),
        shard(4),
        shard(5),
        shard(6),
        grad_up,
        sums[8 * r :],
        after(grad_down, begun_one).astype(F32),
        shard(7),
    )


def solution(mesh):
    rows = P("dp", "ctx", None)
    flags = P("dp", "ctx")
    vector = P(("dp", "ctx"))
    matrix = P(("dp", "ctx"), None)
    in_specs = (
        rows, flags, P(), flags, rows, vector, vector, matrix, vector, matrix,
        matrix, vector, matrix, vector, vector, vector, matrix, vector, matrix, vector,
    )
    out_specs = (
        rows, rows, vector, vector, matrix, vector, matrix, matrix, vector, matrix,
        vector, vector, vector, matrix, vector, matrix, vector,
    )
    return jax.shard_map(local, mesh=mesh, in_specs=in_specs, out_specs=out_specs, check_vma=False)
```

```python
import jax
import jax.numpy as jnp
from jax import lax
from jax.experimental import pallas as pl
from jax.experimental.pallas import tpu as pltpu
from jax.sharding import PartitionSpec as P

HEADS = 32
HEAD_DIM = 64
EPSILON = 1e-05
NEG_FILL = -1e30
SCALE = HEAD_DIM ** (-0.5)
QUERY_BLOCK = 256
BF16 = jnp.bfloat16
F32 = jnp.float32

NN = (((1,), (0,)), ((), ()))
NT = (((1,), (1,)), ((), ()))
TN = (((0,), (0,)), ((), ()))
ANYWHERE = pl.BlockSpec(memory_space=pl.ANY)


def dot(left, right, dims=NN):
    return lax.dot_general(left, right, dims, preferred_element_type=F32)


def forward_kernel(*refs, heads, lanes, block):
    qkv_ref, seg_col_ref, seg_row_ref = refs[:3]
    mixed_ref, log_ref = refs[-2:]
    rows = qkv_ref.shape[0]
    head_of_lane = lax.broadcasted_iota(jnp.int32, (1, lanes), 1) // HEAD_DIM
    diagonal = lax.broadcasted_iota(jnp.int32, (block, block), 1) <= lax.broadcasted_iota(
        jnp.int32, (block, block), 0
    )
    for b in range(rows // block):
        low, high = b * block, (b + 1) * block
        queries = qkv_ref[low:high, :lanes] * jnp.asarray(SCALE, BF16)
        keys = qkv_ref[:high, lanes : 2 * lanes]
        values = qkv_ref[:high, 2 * lanes :]
        allowed = seg_col_ref[low:high, :] == seg_row_ref[:, :high]
        last = allowed[:, low:] & diagonal
        allowed = jnp.concatenate([allowed[:, :low], last], axis=1) if b else last
        mixed = jnp.zeros((block, lanes), F32)
        for h in range(heads):
            mine = head_of_lane == h
            scores = dot(jnp.where(mine, queries, jnp.zeros_like(queries)), keys, NT)
            scores = jnp.where(allowed, scores, NEG_FILL)
            top = jnp.max(scores, axis=1, keepdims=True)
            weights = jnp.exp(scores - top)
            total = jnp.sum(weights, axis=1, keepdims=True)
            product = dot(weights.astype(BF16), values)
            mixed = mixed + jnp.where(mine, product / total, 0.0)
            log_total = jnp.broadcast_to(top + jnp.log(total), (block, 128))
            log_ref[h : h + 1, low:high] = jnp.transpose(log_total)[:1, :]
        mixed_ref[low:high, :] = mixed.astype(BF16)


def backward_kernel(*refs, heads, lanes, block):
    qkv_ref, grad_ref, log_ref, mixed_ref, seg_col_ref, seg_row_ref = refs[:6]
    out_ref, dk_ref, dv_ref = refs[-3:]
    rows = qkv_ref.shape[0]
    head_of_lane = lax.broadcasted_iota(jnp.int32, (1, lanes), 1) // HEAD_DIM
    diagonal = lax.broadcasted_iota(jnp.int32, (block, block), 0) <= lax.broadcasted_iota(
        jnp.int32, (block, block), 1
    )
    scale = jnp.asarray(SCALE, BF16)
    head_rows = jnp.where(lax.broadcasted_iota(jnp.int32, (16, lanes), 0) == head_of_lane, 1.0, 0.0).astype(BF16)
    for b in range(rows // block):
        low, high = b * block, (b + 1) * block
        queries = qkv_ref[low:high, :lanes] * scale
        grads = grad_ref[low:high, :]
        keys = qkv_ref[:high, lanes : 2 * lanes]
        values = qkv_ref[:high, 2 * lanes :]
        allowed = seg_col_ref[:high, :] == seg_row_ref[:, low:high]
        last = allowed[low:, :] & diagonal
        allowed = jnp.concatenate([allowed[:low, :], last], axis=0) if b else last
        products = grads.astype(F32) * mixed_ref[low:high, :].astype(F32)
        coarse = products.astype(BF16)
        fine = (products - coarse.astype(F32)).astype(BF16)
        delta = dot(head_rows, coarse, NT) + dot(head_rows, fine, NT)
        grad_queries = jnp.zeros((block, lanes), F32)
        grad_keys = jnp.zeros((high, lanes), F32)
        grad_values = jnp.zeros((high, lanes), F32)
        for h in range(heads):
            mine = head_of_lane == h
            query_h = jnp.where(mine, queries, jnp.zeros_like(queries))
            grad_h = jnp.where(mine, grads, jnp.zeros_like(grads))
            scores = dot(keys, query_h, NT)
            probs = jnp.where(allowed, jnp.exp(scores - log_ref[h : h + 1, low:high]), 0.0)
            grad_probs = dot(values, grad_h, NT)
            grad_scores = (probs * (grad_probs - delta[h : h + 1, :])).astype(BF16)
            grad_values = grad_values + dot(probs.astype(BF16), grad_h)
            grad_keys = grad_keys + dot(grad_scores, query_h)
            grad_queries = grad_queries + jnp.where(mine, dot(grad_scores, keys, TN), 0.0)
        out_ref[low:high, :lanes] = (grad_queries * SCALE).astype(BF16)
        if b:
            dk_ref[:low, :] = dk_ref[:low, :] + grad_keys[:low, :]
            dv_ref[:low, :] = dv_ref[:low, :] + grad_values[:low, :]
        dk_ref[low:high, :] = grad_keys[low:, :]
        dv_ref[low:high, :] = grad_values[low:, :]
    out_ref[:, lanes : 2 * lanes] = dk_ref[...].astype(BF16)
    out_ref[:, 2 * lanes :] = dv_ref[...].astype(BF16)


def attention_forward(qkv, seg_col, seg_row, earlier):
    rows, lanes = qkv.shape[0], qkv.shape[1] // 3
    heads = lanes // HEAD_DIM
    pairs = rows * rows * heads // 2
    return pl.pallas_call(
        lambda *refs: forward_kernel(*refs, heads=heads, lanes=lanes, block=QUERY_BLOCK),
        out_shape=(jax.ShapeDtypeStruct((rows, lanes), BF16), jax.ShapeDtypeStruct((heads, rows), F32)),
        compiler_params=pltpu.CompilerParams(vmem_limit_bytes=48 * 2**20),
        cost_estimate=pl.CostEstimate(flops=pairs * 5000, bytes_accessed=8 * rows * lanes, transcendentals=pairs),
        in_specs=[pl.BlockSpec(memory_space=pltpu.VMEM)] * 3 + [ANYWHERE] * len(earlier),
        name="attention_forward",
    )(qkv, seg_col, seg_row, *earlier)


def attention_backward(qkv, grads, log_total, mixed, seg_col, seg_row, earlier):
    rows, lanes = qkv.shape[0], qkv.shape[1] // 3
    heads = lanes // HEAD_DIM
    pairs = rows * rows * heads // 2
    return pl.pallas_call(
        lambda *refs: backward_kernel(*refs, heads=heads, lanes=lanes, block=QUERY_BLOCK),
        out_shape=jax.ShapeDtypeStruct((rows, 3 * lanes), BF16),
        scratch_shapes=[pltpu.VMEM((rows, lanes), F32), pltpu.VMEM((rows, lanes), F32)],
        compiler_params=pltpu.CompilerParams(vmem_limit_bytes=48 * 2**20),
        cost_estimate=pl.CostEstimate(flops=pairs * 5000, bytes_accessed=14 * rows * lanes, transcendentals=pairs),
        in_specs=[pl.BlockSpec(memory_space=pltpu.VMEM)] * 6 + [ANYWHERE] * len(earlier),
        name="attention_backward",
    )(qkv, grads, log_total, mixed, seg_col, seg_row, *earlier)


def feed_kernel(normed_ref, grad_ref, up_ref, bias_ref, down_ref, hidden_ref, pre_ref, sum_ref):
    block = 2 * QUERY_BLOCK
    total = jnp.zeros(sum_ref.shape, F32)
    down = jnp.transpose(down_ref[...])
    for low in range(0, normed_ref.shape[0], block):
        rows = slice(low, low + block)
        u = dot(normed_ref[rows, :], up_ref[...]) + bias_ref[...]
        grad_hidden = dot(grad_ref[rows, :], down)
        square = u * u
        bend = jnp.tanh(u * (0.7978845608028654 + (0.7978845608028654 * 0.044715) * square))
        half = 0.5 + 0.5 * bend
        hidden_ref[rows, :] = (u * half).astype(BF16)
        slope = half + u * (half * (1.0 - bend)) * (
            0.7978845608028654 + (3.0 * 0.7978845608028654 * 0.044715) * square
        )
        grad_pre = (grad_hidden * slope).astype(BF16)
        pre_ref[rows, :] = grad_pre
        total = total + jnp.sum(grad_pre.astype(F32), axis=0, keepdims=True)
    sum_ref[...] = total


def feed_forward(normed, grad, w_up, bias, w_down):
    rows, width = normed.shape
    units = w_up.shape[1]
    tile = min(units, 256)
    whole = pl.BlockSpec((rows, width), lambda i: (0, 0))
    column = pl.BlockSpec((rows, tile), lambda i: (0, i))
    line = pl.BlockSpec((1, tile), lambda i: (0, i))
    return pl.pallas_call(
        feed_kernel,
        grid=(units // tile,),
        out_shape=(
            jax.ShapeDtypeStruct((rows, units), BF16),
            jax.ShapeDtypeStruct((rows, units), BF16),
            jax.ShapeDtypeStruct((1, units), F32),
        ),
        in_specs=[
            whole,
            whole,
            pl.BlockSpec((width, tile), lambda i: (0, i)),
            line,
            pl.BlockSpec((tile, width), lambda i: (i, 0)),
        ],
        out_specs=(column, column, line),
        compiler_params=pltpu.CompilerParams(vmem_limit_bytes=56 * 2**20),
        cost_estimate=pl.CostEstimate(
            flops=4 * rows * width * units, bytes_accessed=4 * rows * width, transcendentals=rows * units
        ),
        name="feed_forward",
    )(normed, grad, w_up, bias, w_down)


def chips():
    return lax.axis_size("ctx") // 2


def turn(value, k):
    count = chips()
    return lax.ppermute(
        value, "ctx", [(2 * s + core, 2 * ((s + k) % count) + core) for s in range(count) for core in range(2)]
    )


def swap(value):
    return lax.ppermute(value, "ctx", [(i, i ^ 1) for i in range(2 * chips())])


def place():
    me = lax.axis_index("ctx")
    return me // 2, me % 2


def after(value, *earlier, cost=0):
    def nothing(*refs):
        pass

    return pl.pallas_call(
        nothing,
        out_shape=jax.ShapeDtypeStruct(value.shape, value.dtype),
        in_specs=[ANYWHERE] * (1 + len(earlier)),
        out_specs=ANYWHERE,
        input_output_aliases={0: 0},
        cost_estimate=pl.CostEstimate(flops=cost * 10**9, bytes_accessed=cost * 3 * 10**6, transcendentals=0),
        name="after",
    )(value, *earlier)


def gather_ctx(block):
    count = chips()
    chip, core = place()
    same = [block] + [turn(block, k) for k in range(1, count)]
    chip_of = [(chip + count - k) % count for k in range(count)]
    other = [swap(item) for item in same]
    out = jnp.zeros((2 * count,) + block.shape, block.dtype)
    for k in range(count):
        base = 2 * chip_of[k]
        out = lax.dynamic_update_index_in_dim(out, same[k], base + core, 0)
        out = lax.dynamic_update_index_in_dim(out, other[k], base + 1 - core, 0)
    return out, same[1]


def where_am_i():
    return jnp.stack(place()).astype(jnp.int32)


def pack_columns(weights, cuts, vectors):
    count = chips()
    r = weights[0].shape[0]
    total = sum(lead * width for lead, width in cuts)
    below = -(-len(vectors) // 16) * 16

    def kernel(at_ref, *refs):
        ins, outs = refs[: len(weights)], refs[-(count + 1) :]
        chip, core = at_ref[0], at_ref[1]
        for j in range(2 * count):
            pieces = [
                ref[:, (a * 2 * count + j) * width : (a * 2 * count + j + 1) * width]
                for ref, (lead, width) in zip(ins, cuts)
                for a in range(lead)
            ]
            block = jnp.concatenate(pieces, axis=1)
            slot = lax.rem(j // 2 + count - chip, count)
            for k in range(count):

                @pl.when((slot == k) & (core == j % 2))
                def _(k=k, block=block):
                    outs[k][:r, :] = block

                @pl.when((slot == k) & (core != j % 2))
                def _(k=k, block=block):
                    outs[count][k, :r, :] = block

        if vectors:
            lines = [ref[...].astype(F32) for ref in refs[len(weights) : len(weights) + len(vectors)]]
            lines = [
                jnp.concatenate([line, jnp.zeros((1, total - line.shape[1]), F32)], axis=1) for line in lines
            ]
            more = jnp.concatenate(lines + [jnp.zeros((below - len(lines), total), F32)], axis=0).astype(BF16)
            for k in range(count):
                outs[k][r:, :] = more
                outs[count][k, r:, :] = more

    block_shape = jax.ShapeDtypeStruct((r + below, total), BF16)
    return pl.pallas_call(
        kernel,
        out_shape=[block_shape] * count + [jax.ShapeDtypeStruct((count,) + block_shape.shape, BF16)],
        in_specs=[pl.BlockSpec(memory_space=pltpu.SMEM)]
        + [pl.BlockSpec(memory_space=pltpu.VMEM)] * (len(weights) + len(vectors)),
        name="pack_columns",
    )(where_am_i(), *weights, *vectors)


def pack_rows(arrays, more, height):
    count = chips()
    width = sum(item.shape[1] for item in arrays)
    total = width + more.shape[2]

    def kernel(at_ref, *refs):
        ins, outs = refs[: len(arrays)], refs[-(count + 1) :]
        chip, core = at_ref[0], at_ref[1]
        for k in range(count):
            base = 2 * lax.rem(chip + k, count)
            start = 0
            for ref in ins:
                end = start + ref.shape[1]
                mine = pl.ds(pl.multiple_of((base + core) * height, height), height)
                other = pl.ds(pl.multiple_of((base + 1 - core) * height, height), height)
                outs[k][:, start:end] = ref[mine, :]
                outs[count][k, :, start:end] = ref[other, :]
                start = end
            outs[k][:, width:] = refs[len(arrays)][base + core]
            outs[count][k, :, width:] = refs[len(arrays)][base + 1 - core]

    block_shape = jax.ShapeDtypeStruct((height, total), BF16)
    return pl.pallas_call(
        kernel,
        out_shape=[block_shape] * count + [jax.ShapeDtypeStruct((count,) + block_shape.shape, BF16)],
        in_specs=[pl.BlockSpec(memory_space=pltpu.SMEM)] + [pl.BlockSpec(memory_space=pltpu.VMEM)] * (1 + len(arrays)),
        name="pack_rows",
    )(where_am_i(), *arrays, more)


def exchange_ctx(packed):
    count = chips()
    arrived = swap(packed[count])
    both = [jnp.stack([packed[k], arrived[k]]) for k in range(count)]
    return [both[0]] + [turn(both[k], k) for k in range(1, count)]


def source_index(at_ref, k, side, count):
    core = at_ref[1] if side == 0 else 1 - at_ref[1]
    return 2 * lax.rem(at_ref[0] + count - k, count) + core


def unpack_to_rows(got, r, widths, earlier):
    count = chips()
    height, total = got[0].shape[1:]
    below = height - r

    def kernel(at_ref, *refs):
        ins, outs = refs[:count], refs[count + len(earlier) :]
        for k in range(count):
            for side in range(2):
                index = source_index(at_ref, k, side, count)
                start = 0
                for out, width in zip(outs, widths):
                    out[pl.ds(pl.multiple_of(index * r, r), r), :] = ins[k][side, :r, start : start + width]
                    start += width
                if below:
                    outs[-1][index] = ins[k][side, r:, :]

    return pl.pallas_call(
        kernel,
        out_shape=[jax.ShapeDtypeStruct((2 * count * r, width), BF16) for width in widths]
        + [jax.ShapeDtypeStruct((2 * count, below, total), BF16)] * (below > 0),
        in_specs=[pl.BlockSpec(memory_space=pltpu.SMEM)]
        + [pl.BlockSpec(memory_space=pltpu.VMEM)] * count
        + [ANYWHERE] * len(earlier),
        name="unpack_to_rows",
    )(where_am_i(), *got, *earlier)


def unpack_to_columns(got, cuts, lengths):
    count = chips()
    r, total = got[0].shape[1:]

    def kernel(at_ref, *refs):
        ins, outs, held = refs[:count], refs[count:-1], refs[-1]
        for k in range(count):
            for side in range(2):
                held[source_index(at_ref, k, side, count)] = ins[k][side]
        for j in range(2 * count):
            block = held[j].astype(F32)
            start = 0
            for out, (lead, width) in zip(outs, cuts):
                for a in range(lead):
                    column = (a * 2 * count + j) * width
                    out[:, column : column + width] = block[:, start : start + width]
                    start += width
        added = held[0, :, total - 128 :].astype(F32)
        for j in range(1, 2 * count):
            added = added + held[j, :, total - 128 :].astype(F32)
        lines = jnp.transpose(added)
        columns = sum(lengths) // r
        at = 0
        for out, length in zip(outs[len(cuts) :], lengths):
            parts = [
                lines[i : i + 1, :] + lines[columns + i : columns + i + 1, :] for i in range(at, at + length // r)
            ]
            out[...] = parts[0] if len(parts) == 1 else jnp.concatenate(parts, axis=1)
            at += length // r

    return pl.pallas_call(
        kernel,
        out_shape=[jax.ShapeDtypeStruct((r, 2 * count * lead * width), F32) for lead, width in cuts]
        + [jax.ShapeDtypeStruct((1, length), F32) for length in lengths],
        in_specs=[pl.BlockSpec(memory_space=pltpu.SMEM)] + [pl.BlockSpec(memory_space=pltpu.VMEM)] * count,
        scratch_shapes=[pltpu.VMEM((2 * count, r, total), BF16)],
        name="unpack_to_columns",
    )(where_am_i(), *got)


def split_rows(rows):
    count = chips()
    chip, core = place()
    pairs = rows.reshape((count, 2, rows.shape[0] // (2 * count), rows.shape[1]))
    order = [(chip + k) % count for k in range(1, count + 1)]
    turned = [lax.dynamic_index_in_dim(pairs, index, 0, keepdims=False) for index in order]
    pick = lambda which: jnp.concatenate(
        [lax.dynamic_index_in_dim(item, which, 0, keepdims=False) for item in turned], axis=0
    )
    return pick(core), pick(1 - core)


def chip_sums(left, right, dims, earlier=()):
    count = chips()
    mine, other = split_rows(left)
    leaving = dot(other, right, dims).astype(BF16)
    arrived = swap(after(leaving, *earlier) if earlier else leaving)
    own = dot(mine, right, dims)
    n = own.shape[0] // count
    sums = [own[k * n : (k + 1) * n] + arrived[k * n : (k + 1) * n].astype(F32) for k in range(count)]
    return [item.astype(BF16) for item in sums[:-1]] + sums[-1:]


def add_over_chips(sums, earlier=()):
    count = chips()
    total = sums[-1]
    for k in range(1, count):
        arrived = turn(sums[k - 1], k)
        arrived = after(arrived, *earlier) if earlier else arrived
        total = total + arrived.astype(F32)
        first = arrived if k == 1 else first
    return total, first


def reduce_dp_small(blocks):
    parts = lax.axis_size("dp")
    me = lax.axis_index("dp")
    total = lax.dynamic_index_in_dim(blocks, me, 0, keepdims=False)
    for k in range(1, parts):
        piece = lax.dynamic_index_in_dim(blocks, (me + k) % parts, 0, keepdims=False)
        total = total + lax.ppermute(piece, "dp", [(i, (i + k) % parts) for i in range(parts)])
    return total


def gather_dp(value):
    return lax.all_gather(value, "dp", axis=0, tiled=True)


def scatter_dp(value):
    return lax.psum_scatter(value, "dp", scatter_dimension=0, tiled=True)


def across(value, k):
    return lax.ppermute(value, "dp", [(i, i ^ k) for i in range(lax.axis_size("dp"))])


def turn_gather_dp(value):
    parts = lax.axis_size("dp")
    me = lax.axis_index("dp")
    out = jnp.zeros((parts,) + value.shape, value.dtype)
    out = lax.dynamic_update_index_in_dim(out, value, me, 0)
    for k in range(1, parts):
        out = lax.dynamic_update_index_in_dim(out, across(value, k), me ^ k, 0)
    return out.reshape((parts * value.shape[0],) + value.shape[1:])


def turn_scatter_dp(blocks):
    parts = lax.axis_size("dp")
    me = lax.axis_index("dp")
    blocks = blocks.reshape((parts, blocks.shape[0] // parts) + blocks.shape[1:])
    total = lax.dynamic_index_in_dim(blocks, me, 0, keepdims=False).astype(F32)
    for k in range(1, parts):
        total = total + across(lax.dynamic_index_in_dim(blocks, me ^ k, 0, keepdims=False), k).astype(F32)
    return total


def standardize(values):
    average = jnp.mean(values, axis=-1, keepdims=True)
    centered = values - average
    variance = jnp.mean(centered * centered, axis=-1, keepdims=True)
    factor = lax.rsqrt(variance + EPSILON)
    return centered * factor, factor


def norm_back(grad, gain, standard, factor):
    scaled = grad * gain
    return (
        scaled
        - jnp.mean(scaled, axis=-1, keepdims=True)
        - standard * jnp.mean(scaled * standard, axis=-1, keepdims=True)
    ) * factor


def local(
    tokens_in,
    exit_layer,
    layer_index,
    segment_ids,
    grad_out,
    first_gain,
    first_bias,
    query_weight,
    query_bias,
    key_weight,
    value_weight,
    value_bias,
    out_weight,
    out_bias,
    second_gain,
    second_bias,
    up_weight,
    up_bias,
    down_weight,
    down_bias,
):
    T, N = lax.axis_size("ctx"), lax.axis_size("dp")
    me = lax.axis_index("ctx")
    n, D = tokens_in.shape[1], tokens_in.shape[2]
    r = first_gain.shape[0]
    f = up_bias.shape[0]
    S = T * n
    B = max(HEAD_DIM, r)
    A = D // (T * B)
    L = A * B
    x = tokens_in[0]
    g_out = grad_out[0]
    active = (exit_layer[0] > layer_index[0]).astype(F32)

    x_all = lax.all_gather(x, "ctx", axis=0, tiled=True)
    natural = r % HEAD_DIM == 0
    if natural:
        w_out = turn_gather_dp(out_weight)
    else:
        w_all = lax.all_gather(out_weight, ("dp", "ctx"), axis=0, tiled=True).reshape(A, T, B, D)
        w_out = lax.dynamic_index_in_dim(w_all, me, 1, keepdims=False).reshape(L, D)
    vectors = [first_gain, first_bias, query_bias, value_bias, out_bias, second_gain, second_bias, down_bias, up_bias]
    vectors = [v.reshape(1, -1) for v in vectors + [active.astype(BF16), segment_ids[0].astype(BF16)]]
    got = exchange_ctx(pack_columns([query_weight, key_weight, value_weight], [(A, B)] * 3, vectors))
    qkv_rows, small_got = unpack_to_rows(got, r, (3 * L,), (x_all, w_out))
    up_packed = pack_columns([up_weight], [(N, f)], [])
    w_qkv = gather_dp(qkv_rows)
    small_width = max(r, f)
    params = turn_gather_dp(small_got[:, :9, :small_width].reshape(T * 9, small_width)).reshape(N, T, 9, small_width)
    g_all, g_begun = gather_ctx(after(g_out, qkv_rows))
    g_all = g_all.reshape(S, D)

    feature = lambda i: params[:, :, i, :r].reshape(D).astype(F32)
    gain_one, bias_one, bias_query, bias_value, bias_out, gain_two, bias_two, bias_down = (
        feature(i) for i in range(8)
    )
    bias_up = lax.dynamic_index_in_dim(params[:, :, 8, :f], me, 1, keepdims=False).reshape(N * f).astype(F32)
    active_row = small_got[:, 9, :n].reshape(S)
    segs = small_got[:, 10, :n].reshape(S).astype(jnp.int32)
    seg_col, seg_row = segs.reshape(S, 1), segs.reshape(1, S)
    own_heads = lambda v: lax.dynamic_index_in_dim(v.reshape(A, T, B), me, 1, keepdims=False).reshape(L)
    bias_qkv = jnp.concatenate([own_heads(bias_query), jnp.zeros((L,), F32), own_heads(bias_value)])

    standard_one, _ = standardize(x_all.astype(F32))
    normed_one = after((standard_one * gain_one + bias_one).astype(BF16), g_all)
    qkv = (dot(normed_one, w_qkv) + bias_qkv).astype(BF16)
    w_down = gather_dp(after(down_weight, qkv))
    up_got = exchange_ctx([*up_packed[:-1], after(up_packed[-1], g_begun)])
    mixed, log_total = attention_forward(qkv, seg_col, seg_row, ())
    (up_rows,) = unpack_to_rows(up_got, r, (N * f,), (mixed,))
    w_up = gather_dp(up_rows)
    branch = add_over_chips(chip_sums(mixed, w_out, NN, (up_rows,)))[0] + bias_out
    inputs = x.astype(F32)
    active_own = active[:, None]
    middle = inputs + active_own * branch

    standard_two, factor_two = standardize(middle)
    normed_two = (standard_two * gain_two + bias_two).astype(BF16)
    normed_two_all = gather_ctx(after(normed_two, cost=0))[0].reshape(S, D)
    grad_ffn = (active_row[:, None] * g_all).astype(BF16)
    hidden, grad_pre, grad_up_sum = feed_forward(normed_two_all, grad_ffn, w_up, bias_up.reshape(1, N * f), w_down)
    sums_two = chip_sums(grad_pre, w_up, NT)
    grad_normed_two, begun_two = add_over_chips(sums_two)
    hidden = after(hidden, sums_two[0])
    grad_down_part = dot(hidden, grad_ffn, TN).astype(BF16)
    grad_down = scatter_dp(grad_down_part)
    grad_up_part = dot(after(normed_two_all, sums_two[0]), grad_pre, TN).astype(BF16)
    grad_up_mine = scatter_dp(grad_up_part)
    feed_sums = chip_sums(after(hidden, begun_two), w_down, NN)
    grad_res = g_out.astype(F32)
    grad_middle = grad_res + norm_back(grad_normed_two, gain_two, standard_two, factor_two)
    grad_branch = after((active_own * grad_middle).astype(BF16), cost=250)

    grad_branch_all = gather_ctx(grad_branch)[0].reshape(S, D)
    grad_heads = dot(grad_branch_all, w_out, NT).astype(BF16)
    grad_out_w = dot(mixed, grad_branch_all, TN)
    if natural:
        grad_out_w = scatter_dp(grad_out_w.astype(BF16))
    else:
        spread = jnp.zeros((A, T, B, D), F32)
        spread = lax.dynamic_update_index_in_dim(spread, grad_out_w.reshape(A, B, D), me, 1)
        grad_out_w = lax.psum_scatter(spread.reshape(D, D), ("dp", "ctx"), scatter_dimension=0, tiled=True)
    grad_qkv = attention_backward(
        qkv, grad_heads, log_total, mixed, seg_col, seg_row, (grad_down, grad_up_mine)
    )

    grad_qkv_part = dot(normed_one, grad_qkv, TN).astype(BF16)
    feed, _ = add_over_chips([after(item, grad_branch_all) for item in feed_sums[:-1]] + feed_sums[-1:], (grad_qkv,))
    sums_one = chip_sums(grad_qkv, w_qkv, NT, (grad_qkv_part, feed, grad_out_w))
    grad_normed_one, begun_one = add_over_chips(sums_one)
    grad_normed_one = after(grad_normed_one, cost=0)
    layer_out = (middle + active_own * (feed + bias_down)).astype(BF16)[None]
    standard_in, factor_in = standardize(inputs)
    grad_in = (grad_middle + norm_back(grad_normed_one, gain_one, standard_in, factor_in)).astype(BF16)[None]

    partial_one = dot(after(grad_qkv, begun_one), w_qkv, NT)
    grad_gain_one = jnp.sum(partial_one * standard_one, axis=0)
    grad_bias_one = jnp.sum(partial_one, axis=0)
    grad_gain_two = jnp.sum(grad_normed_two * standard_two, axis=0)
    grad_bias_two = jnp.sum(grad_normed_two, axis=0)
    ctx_index = lax.broadcasted_iota(jnp.int32, (1, T, 1), 1)
    spread_heads = lambda v: jnp.where(ctx_index == me, v.reshape(A, 1, B), 0.0).reshape(D)
    grad_bias_qkv = jnp.sum(grad_qkv.astype(F32), axis=0)
    grad_out_sum = jnp.sum(grad_branch.astype(F32), axis=0)
    grad_down_sum = jnp.sum((active_own * grad_res), axis=0)
    features = jnp.stack(
        [
            grad_gain_one,
            grad_bias_one,
            spread_heads(grad_bias_qkv[:L]),
            spread_heads(grad_bias_qkv[2 * L :]),
            grad_out_sum,
            grad_gain_two,
            grad_bias_two,
            grad_down_sum,
        ]
    )
    features = features.reshape(8, N, T, r).transpose(1, 2, 0, 3).reshape(N, T, 8 * r)
    units = jnp.where(
        lax.broadcasted_iota(jnp.int32, (1, T, 1), 1) == me, grad_up_sum.reshape(N, 1, f), 0.0
    )
    sums = jnp.concatenate([features, units], axis=2).reshape(N, T * (8 * r + f))
    sums = reduce_dp_small(sums).reshape(T, 8 * r + f)
    grad_qkv_mine = scatter_dp(grad_qkv_part)
    sums = sums.reshape(T, 8 + f // r, r).transpose(0, 2, 1)
    coarse = sums.astype(BF16)
    fine = (sums - coarse.astype(F32)).astype(BF16)
    more = jnp.pad(jnp.concatenate([coarse, fine], axis=2), ((0, 0), (0, 0), (0, 128 - 2 * sums.shape[2])))
    grad_got = exchange_ctx(pack_rows([after(grad_qkv_mine, grad_normed_one), grad_up_mine], more, r))
    grad_q, grad_k, grad_v, grad_up, *lines = unpack_to_columns(grad_got, [(A, B)] * 3 + [(N, f)], [r] * 8 + [f])
    shard = lambda i: lines[i].reshape(-1)
    return (
        layer_out,
        grad_in,
        shard(0),
        shard(1),
        grad_q,
        shard(2),
        grad_k,
        grad_v,
        shard(3),
        grad_out_w.astype(F32),
        shard(4),
        shard(5),
        shard(6),
        grad_up,
        shard(8),
        after(grad_down, grad_got[0]).astype(F32),
        shard(7),
    )


def solution(mesh):
    rows = P("dp", "ctx", None)
    flags = P("dp", "ctx")
    vector = P(("dp", "ctx"))
    matrix = P(("dp", "ctx"), None)
    in_specs = (
        rows, flags, P(), flags, rows, vector, vector, matrix, vector, matrix,
        matrix, vector, matrix, vector, vector, vector, matrix, vector, matrix, vector,
    )
    out_specs = (
        rows, rows, vector, vector, matrix, vector, matrix, matrix, vector, matrix,
        vector, vector, vector, matrix, vector, matrix, vector,
    )
    return jax.shard_map(local, mesh=mesh, in_specs=in_specs, out_specs=out_specs, check_vma=False)
```

```python
import jax
import jax.numpy as jnp
from jax import lax
from jax.experimental import pallas as pl
from jax.experimental.pallas import tpu as pltpu
from jax.sharding import PartitionSpec as P

HEADS = 32
HEAD_DIM = 64
EPSILON = 1e-05
NEG_FILL = -1e30
SCALE = HEAD_DIM ** (-0.5)
QUERY_BLOCK = 256
BF16 = jnp.bfloat16
F32 = jnp.float32

NN = (((1,), (0,)), ((), ()))
NT = (((1,), (1,)), ((), ()))
TN = (((0,), (0,)), ((), ()))
ANYWHERE = pl.BlockSpec(memory_space=pl.ANY)


def dot(left, right, dims=NN):
    return lax.dot_general(left, right, dims, preferred_element_type=F32)


def forward_kernel(*refs, heads, lanes, block):
    qkv_ref, seg_col_ref, seg_row_ref = refs[:3]
    mixed_ref, log_ref = refs[-2:]
    rows = qkv_ref.shape[0]
    head_of_lane = lax.broadcasted_iota(jnp.int32, (1, lanes), 1) // HEAD_DIM
    diagonal = lax.broadcasted_iota(jnp.int32, (block, block), 1) <= lax.broadcasted_iota(
        jnp.int32, (block, block), 0
    )
    for b in range(rows // block):
        low, high = b * block, (b + 1) * block
        queries = qkv_ref[low:high, :lanes] * jnp.asarray(SCALE, BF16)
        keys = qkv_ref[:high, lanes : 2 * lanes]
        values = qkv_ref[:high, 2 * lanes :]
        allowed = seg_col_ref[low:high, :] == seg_row_ref[:, :high]
        last = allowed[:, low:] & diagonal
        allowed = jnp.concatenate([allowed[:, :low], last], axis=1) if b else last
        mixed = jnp.zeros((block, lanes), F32)
        for h in range(heads):
            mine = head_of_lane == h
            scores = dot(jnp.where(mine, queries, jnp.zeros_like(queries)), keys, NT)
            scores = jnp.where(allowed, scores, NEG_FILL)
            top = jnp.max(scores, axis=1, keepdims=True)
            weights = jnp.exp(scores - top)
            total = jnp.sum(weights, axis=1, keepdims=True)
            product = dot(weights.astype(BF16), values)
            mixed = mixed + jnp.where(mine, product / total, 0.0)
            log_total = jnp.broadcast_to(top + jnp.log(total), (block, 128))
            log_ref[h : h + 1, low:high] = jnp.transpose(log_total)[:1, :]
        mixed_ref[low:high, :] = mixed.astype(BF16)


def backward_kernel(*refs, heads, lanes, block):
    qkv_ref, grad_ref, log_ref, mixed_ref, seg_col_ref, seg_row_ref = refs[:6]
    out_ref, dk_ref, dv_ref = refs[-3:]
    rows = qkv_ref.shape[0]
    head_of_lane = lax.broadcasted_iota(jnp.int32, (1, lanes), 1) // HEAD_DIM
    diagonal = lax.broadcasted_iota(jnp.int32, (block, block), 0) <= lax.broadcasted_iota(
        jnp.int32, (block, block), 1
    )
    scale = jnp.asarray(SCALE, BF16)
    head_rows = jnp.where(lax.broadcasted_iota(jnp.int32, (16, lanes), 0) == head_of_lane, 1.0, 0.0).astype(BF16)
    for b in range(rows // block):
        low, high = b * block, (b + 1) * block
        queries = qkv_ref[low:high, :lanes] * scale
        grads = grad_ref[low:high, :]
        keys = qkv_ref[:high, lanes : 2 * lanes]
        values = qkv_ref[:high, 2 * lanes :]
        allowed = seg_col_ref[:high, :] == seg_row_ref[:, low:high]
        last = allowed[low:, :] & diagonal
        allowed = jnp.concatenate([allowed[:low, :], last], axis=0) if b else last
        products = grads.astype(F32) * mixed_ref[low:high, :].astype(F32)
        coarse = products.astype(BF16)
        fine = (products - coarse.astype(F32)).astype(BF16)
        delta = dot(head_rows, coarse, NT) + dot(head_rows, fine, NT)
        grad_queries = jnp.zeros((block, lanes), F32)
        grad_keys = jnp.zeros((high, lanes), F32)
        grad_values = jnp.zeros((high, lanes), F32)
        for h in range(heads):
            mine = head_of_lane == h
            query_h = jnp.where(mine, queries, jnp.zeros_like(queries))
            grad_h = jnp.where(mine, grads, jnp.zeros_like(grads))
            scores = dot(keys, query_h, NT)
            probs = jnp.where(allowed, jnp.exp(scores - log_ref[h : h + 1, low:high]), 0.0)
            grad_probs = dot(values, grad_h, NT)
            grad_scores = (probs * (grad_probs - delta[h : h + 1, :])).astype(BF16)
            grad_values = grad_values + dot(probs.astype(BF16), grad_h)
            grad_keys = grad_keys + dot(grad_scores, query_h)
            grad_queries = grad_queries + jnp.where(mine, dot(grad_scores, keys, TN), 0.0)
        out_ref[low:high, :lanes] = (grad_queries * SCALE).astype(BF16)
        if b:
            dk_ref[:low, :] = dk_ref[:low, :] + grad_keys[:low, :]
            dv_ref[:low, :] = dv_ref[:low, :] + grad_values[:low, :]
        dk_ref[low:high, :] = grad_keys[low:, :]
        dv_ref[low:high, :] = grad_values[low:, :]
    out_ref[:, lanes : 2 * lanes] = dk_ref[...].astype(BF16)
    out_ref[:, 2 * lanes :] = dv_ref[...].astype(BF16)


def attention_forward(qkv, seg_col, seg_row, earlier):
    rows, lanes = qkv.shape[0], qkv.shape[1] // 3
    heads = lanes // HEAD_DIM
    pairs = rows * rows * heads // 2
    return pl.pallas_call(
        lambda *refs: forward_kernel(*refs, heads=heads, lanes=lanes, block=QUERY_BLOCK),
        out_shape=(jax.ShapeDtypeStruct((rows, lanes), BF16), jax.ShapeDtypeStruct((heads, rows), F32)),
        compiler_params=pltpu.CompilerParams(vmem_limit_bytes=48 * 2**20),
        cost_estimate=pl.CostEstimate(flops=pairs * 5000, bytes_accessed=8 * rows * lanes, transcendentals=pairs),
        in_specs=[pl.BlockSpec(memory_space=pltpu.VMEM)] * 3 + [ANYWHERE] * len(earlier),
        name="attention_forward",
    )(qkv, seg_col, seg_row, *earlier)


def attention_backward(qkv, grads, log_total, mixed, seg_col, seg_row, earlier):
    rows, lanes = qkv.shape[0], qkv.shape[1] // 3
    heads = lanes // HEAD_DIM
    pairs = rows * rows * heads // 2
    return pl.pallas_call(
        lambda *refs: backward_kernel(*refs, heads=heads, lanes=lanes, block=QUERY_BLOCK),
        out_shape=jax.ShapeDtypeStruct((rows, 3 * lanes), BF16),
        scratch_shapes=[pltpu.VMEM((rows, lanes), F32), pltpu.VMEM((rows, lanes), F32)],
        compiler_params=pltpu.CompilerParams(vmem_limit_bytes=48 * 2**20),
        cost_estimate=pl.CostEstimate(flops=pairs * 5000, bytes_accessed=14 * rows * lanes, transcendentals=pairs),
        in_specs=[pl.BlockSpec(memory_space=pltpu.VMEM)] * 6 + [ANYWHERE] * len(earlier),
        name="attention_backward",
    )(qkv, grads, log_total, mixed, seg_col, seg_row, *earlier)


def feed_kernel(normed_ref, grad_ref, up_ref, bias_ref, down_ref, hidden_ref, pre_ref, sum_ref):
    block = 2 * QUERY_BLOCK
    total = jnp.zeros(sum_ref.shape, F32)
    down = jnp.transpose(down_ref[...])
    for low in range(0, normed_ref.shape[0], block):
        rows = slice(low, low + block)
        u = dot(normed_ref[rows, :], up_ref[...]) + bias_ref[...]
        grad_hidden = dot(grad_ref[rows, :], down)
        square = u * u
        bend = jnp.tanh(u * (0.7978845608028654 + (0.7978845608028654 * 0.044715) * square))
        half = 0.5 + 0.5 * bend
        hidden_ref[rows, :] = (u * half).astype(BF16)
        slope = half + u * (half * (1.0 - bend)) * (
            0.7978845608028654 + (3.0 * 0.7978845608028654 * 0.044715) * square
        )
        grad_pre = (grad_hidden * slope).astype(BF16)
        pre_ref[rows, :] = grad_pre
        total = total + jnp.sum(grad_pre.astype(F32), axis=0, keepdims=True)
    sum_ref[...] = total


def feed_forward(normed, grad, w_up, bias, w_down):
    rows, width = normed.shape
    units = w_up.shape[1]
    tile = min(units, 256)
    whole = pl.BlockSpec((rows, width), lambda i: (0, 0))
    column = pl.BlockSpec((rows, tile), lambda i: (0, i))
    line = pl.BlockSpec((1, tile), lambda i: (0, i))
    return pl.pallas_call(
        feed_kernel,
        grid=(units // tile,),
        out_shape=(
            jax.ShapeDtypeStruct((rows, units), BF16),
            jax.ShapeDtypeStruct((rows, units), BF16),
            jax.ShapeDtypeStruct((1, units), F32),
        ),
        in_specs=[
            whole,
            whole,
            pl.BlockSpec((width, tile), lambda i: (0, i)),
            line,
            pl.BlockSpec((tile, width), lambda i: (i, 0)),
        ],
        out_specs=(column, column, line),
        compiler_params=pltpu.CompilerParams(vmem_limit_bytes=56 * 2**20),
        cost_estimate=pl.CostEstimate(
            flops=4 * rows * width * units, bytes_accessed=4 * rows * width, transcendentals=rows * units
        ),
        name="feed_forward",
    )(normed, grad, w_up, bias, w_down)


def chips():
    return lax.axis_size("ctx") // 2


def turn(value, k):
    count = chips()
    return lax.ppermute(
        value, "ctx", [(2 * s + core, 2 * ((s + k) % count) + core) for s in range(count) for core in range(2)]
    )


FAR = ((0, 2), (1, 3), (2, 0), (3, 1))
NEAR = ((0, 1), (1, 0), (2, 3), (3, 2))
MIDDLE = ((1, 2), (2, 1))
OUT = ((2, 3), (1, 0))
BACK = ((3, 2), (0, 1))


def chip_permute(value, pairs):
    return lax.ppermute(value, "ctx", [(2 * s + core, 2 * t + core) for s, t in pairs for core in range(2)])


def swap(value):
    return lax.ppermute(value, "ctx", [(i, i ^ 1) for i in range(2 * chips())])


def place():
    me = lax.axis_index("ctx")
    return me // 2, me % 2


def after(value, *earlier, cost=0):
    def nothing(*refs):
        pass

    return pl.pallas_call(
        nothing,
        out_shape=jax.ShapeDtypeStruct(value.shape, value.dtype),
        in_specs=[ANYWHERE] * (1 + len(earlier)),
        out_specs=ANYWHERE,
        input_output_aliases={0: 0},
        cost_estimate=pl.CostEstimate(flops=cost * 10**9, bytes_accessed=cost * 3 * 10**6, transcendentals=0),
        name="after",
    )(value, *earlier)


def gather_ctx(block):
    count = chips()
    chip, core = place()
    if count == 4:
        far, near, middle = (chip_permute(block, pairs) for pairs in (FAR, NEAR, MIDDLE))
        last = jnp.where((chip == 0) | (chip == 3), chip_permute(far, OUT), middle)
        same, chip_of = [block, near, far, last], [chip, chip ^ 1, chip ^ 2, chip ^ 3]
    else:
        same = [block] + [turn(block, k) for k in range(1, count)]
        chip_of = [(chip + count - k) % count for k in range(count)]
    other = [swap(item) for item in same]
    out = jnp.zeros((2 * count,) + block.shape, block.dtype)
    for k in range(count):
        base = 2 * chip_of[k]
        out = lax.dynamic_update_index_in_dim(out, same[k], base + core, 0)
        out = lax.dynamic_update_index_in_dim(out, other[k], base + 1 - core, 0)
    return out, same[1]


def where_am_i():
    return jnp.stack(place()).astype(jnp.int32)


def pack_columns(weights, cuts, vectors):
    count = chips()
    r = weights[0].shape[0]
    total = sum(lead * width for lead, width in cuts)
    below = -(-len(vectors) // 16) * 16

    def kernel(at_ref, *refs):
        ins, outs = refs[: len(weights)], refs[-(count + 1) :]
        chip, core = at_ref[0], at_ref[1]
        for j in range(2 * count):
            pieces = [
                ref[:, (a * 2 * count + j) * width : (a * 2 * count + j + 1) * width]
                for ref, (lead, width) in zip(ins, cuts)
                for a in range(lead)
            ]
            block = jnp.concatenate(pieces, axis=1)
            slot = lax.rem(j // 2 + count - chip, count)
            for k in range(count):

                @pl.when((slot == k) & (core == j % 2))
                def _(k=k, block=block):
                    outs[k][:r, :] = block

                @pl.when((slot == k) & (core != j % 2))
                def _(k=k, block=block):
                    outs[count][k, :r, :] = block

        if vectors:
            lines = [ref[...].astype(F32) for ref in refs[len(weights) : len(weights) + len(vectors)]]
            lines = [
                jnp.concatenate([line, jnp.zeros((1, total - line.shape[1]), F32)], axis=1) for line in lines
            ]
            more = jnp.concatenate(lines + [jnp.zeros((below - len(lines), total), F32)], axis=0).astype(BF16)
            for k in range(count):
                outs[k][r:, :] = more
                outs[count][k, r:, :] = more

    block_shape = jax.ShapeDtypeStruct((r + below, total), BF16)
    return pl.pallas_call(
        kernel,
        out_shape=[block_shape] * count + [jax.ShapeDtypeStruct((count,) + block_shape.shape, BF16)],
        in_specs=[pl.BlockSpec(memory_space=pltpu.SMEM)]
        + [pl.BlockSpec(memory_space=pltpu.VMEM)] * (len(weights) + len(vectors)),
        name="pack_columns",
    )(where_am_i(), *weights, *vectors)


def pack_rows(arrays, more, height):
    count = chips()
    width = sum(item.shape[1] for item in arrays)
    total = width + more.shape[2]

    def kernel(at_ref, *refs):
        ins, outs = refs[: len(arrays)], refs[-(count + 1) :]
        chip, core = at_ref[0], at_ref[1]
        for k in range(count):
            base = 2 * lax.rem(chip + k, count)
            start = 0
            for ref in ins:
                end = start + ref.shape[1]
                mine = pl.ds(pl.multiple_of((base + core) * height, height), height)
                other = pl.ds(pl.multiple_of((base + 1 - core) * height, height), height)
                outs[k][:, start:end] = ref[mine, :]
                outs[count][k, :, start:end] = ref[other, :]
                start = end
            outs[k][:, width:] = refs[len(arrays)][base + core]
            outs[count][k, :, width:] = refs[len(arrays)][base + 1 - core]

    block_shape = jax.ShapeDtypeStruct((height, total), BF16)
    return pl.pallas_call(
        kernel,
        out_shape=[block_shape] * count + [jax.ShapeDtypeStruct((count,) + block_shape.shape, BF16)],
        in_specs=[pl.BlockSpec(memory_space=pltpu.SMEM)] + [pl.BlockSpec(memory_space=pltpu.VMEM)] * (1 + len(arrays)),
        name="pack_rows",
    )(where_am_i(), *arrays, more)


def exchange_ctx(packed):
    count = chips()
    arrived = swap(packed[count])
    both = [jnp.stack([packed[k], arrived[k]]) for k in range(count)]
    return [both[0]] + [turn(both[k], k) for k in range(1, count)]


def source_index(at_ref, k, side, count):
    core = at_ref[1] if side == 0 else 1 - at_ref[1]
    return 2 * lax.rem(at_ref[0] + count - k, count) + core


def unpack_to_rows(got, r, widths, earlier):
    count = chips()
    height, total = got[0].shape[1:]
    below = height - r

    def kernel(at_ref, *refs):
        ins, outs = refs[:count], refs[count + len(earlier) :]
        for k in range(count):
            for side in range(2):
                index = source_index(at_ref, k, side, count)
                start = 0
                for out, width in zip(outs, widths):
                    out[pl.ds(pl.multiple_of(index * r, r), r), :] = ins[k][side, :r, start : start + width]
                    start += width
                if below:
                    outs[-1][index] = ins[k][side, r:, :]

    return pl.pallas_call(
        kernel,
        out_shape=[jax.ShapeDtypeStruct((2 * count * r, width), BF16) for width in widths]
        + [jax.ShapeDtypeStruct((2 * count, below, total), BF16)] * (below > 0),
        in_specs=[pl.BlockSpec(memory_space=pltpu.SMEM)]
        + [pl.BlockSpec(memory_space=pltpu.VMEM)] * count
        + [ANYWHERE] * len(earlier),
        name="unpack_to_rows",
    )(where_am_i(), *got, *earlier)


def unpack_to_columns(got, cuts, lengths):
    count = chips()
    r, total = got[0].shape[1:]

    def kernel(at_ref, *refs):
        ins, outs, held = refs[:count], refs[count:-1], refs[-1]
        for k in range(count):
            for side in range(2):
                held[source_index(at_ref, k, side, count)] = ins[k][side]
        for j in range(2 * count):
            block = held[j].astype(F32)
            start = 0
            for out, (lead, width) in zip(outs, cuts):
                for a in range(lead):
                    column = (a * 2 * count + j) * width
                    out[:, column : column + width] = block[:, start : start + width]
                    start += width
        added = held[0, :, total - 128 :].astype(F32)
        for j in range(1, 2 * count):
            added = added + held[j, :, total - 128 :].astype(F32)
        lines = jnp.transpose(added)
        columns = sum(lengths) // r
        at = 0
        for out, length in zip(outs[len(cuts) :], lengths):
            parts = [
                lines[i : i + 1, :] + lines[columns + i : columns + i + 1, :] for i in range(at, at + length // r)
            ]
            out[...] = parts[0] if len(parts) == 1 else jnp.concatenate(parts, axis=1)
            at += length // r

    return pl.pallas_call(
        kernel,
        out_shape=[jax.ShapeDtypeStruct((r, 2 * count * lead * width), F32) for lead, width in cuts]
        + [jax.ShapeDtypeStruct((1, length), F32) for length in lengths],
        in_specs=[pl.BlockSpec(memory_space=pltpu.SMEM)] + [pl.BlockSpec(memory_space=pltpu.VMEM)] * count,
        scratch_shapes=[pltpu.VMEM((2 * count, r, total), BF16)],
        name="unpack_to_columns",
    )(where_am_i(), *got)


def split_rows(rows):
    count = chips()
    chip, core = place()
    pairs = rows.reshape((count, 2, rows.shape[0] // (2 * count), rows.shape[1]))
    order = [chip ^ (3 - k) for k in range(4)] if count == 4 else [(chip + k) % count for k in range(1, count + 1)]
    turned = [lax.dynamic_index_in_dim(pairs, index, 0, keepdims=False) for index in order]
    pick = lambda which: jnp.concatenate(
        [lax.dynamic_index_in_dim(item, which, 0, keepdims=False) for item in turned], axis=0
    )
    return pick(core), pick(1 - core)


def chip_sums(left, right, dims, earlier=()):
    count = chips()
    mine, other = split_rows(left)
    leaving = dot(other, right, dims).astype(BF16)
    arrived = swap(after(leaving, *earlier) if earlier else leaving)
    own = dot(mine, right, dims)
    n = own.shape[0] // count
    sums = [own[k * n : (k + 1) * n] + arrived[k * n : (k + 1) * n].astype(F32) for k in range(count)]
    return [item.astype(BF16) for item in sums[:-1]] + sums[-1:]


def add_over_chips(sums, earlier=()):
    count = chips()
    total = sums[-1]
    if count == 4:
        ends, middle, near = (chip_permute(*pair) for pair in ((sums[0], BACK), (sums[0], MIDDLE), (sums[2], NEAR)))
        far = chip_permute((sums[1].astype(F32) + ends.astype(F32)).astype(BF16), FAR)
        for arrived in (middle, near, far):
            arrived = after(arrived, *earlier) if earlier else arrived
            total = total + arrived.astype(F32)
        return total, near
    for k in range(1, count):
        arrived = turn(sums[k - 1], k)
        arrived = after(arrived, *earlier) if earlier else arrived
        total = total + arrived.astype(F32)
        first = arrived if k == 1 else first
    return total, first


def reduce_dp_small(blocks):
    parts = lax.axis_size("dp")
    me = lax.axis_index("dp")
    total = lax.dynamic_index_in_dim(blocks, me, 0, keepdims=False)
    for k in range(1, parts):
        piece = lax.dynamic_index_in_dim(blocks, (me + k) % parts, 0, keepdims=False)
        total = total + lax.ppermute(piece, "dp", [(i, (i + k) % parts) for i in range(parts)])
    return total


def gather_dp(value):
    return lax.all_gather(value, "dp", axis=0, tiled=True)


def scatter_dp(value):
    return lax.psum_scatter(value, "dp", scatter_dimension=0, tiled=True)


def across(value, k):
    return lax.ppermute(value, "dp", [(i, i ^ k) for i in range(lax.axis_size("dp"))])


def turn_gather_dp(value):
    parts = lax.axis_size("dp")
    me = lax.axis_index("dp")
    out = jnp.zeros((parts,) + value.shape, value.dtype)
    out = lax.dynamic_update_index_in_dim(out, value, me, 0)
    for k in range(1, parts):
        out = lax.dynamic_update_index_in_dim(out, across(value, k), me ^ k, 0)
    return out.reshape((parts * value.shape[0],) + value.shape[1:])


def turn_scatter_dp(blocks):
    parts = lax.axis_size("dp")
    me = lax.axis_index("dp")
    blocks = blocks.reshape((parts, blocks.shape[0] // parts) + blocks.shape[1:])
    total = lax.dynamic_index_in_dim(blocks, me, 0, keepdims=False).astype(F32)
    for k in range(1, parts):
        total = total + across(lax.dynamic_index_in_dim(blocks, me ^ k, 0, keepdims=False), k).astype(F32)
    return total


def standardize(values):
    average = jnp.mean(values, axis=-1, keepdims=True)
    centered = values - average
    variance = jnp.mean(centered * centered, axis=-1, keepdims=True)
    factor = lax.rsqrt(variance + EPSILON)
    return centered * factor, factor


def norm_back(grad, gain, standard, factor):
    scaled = grad * gain
    return (
        scaled
        - jnp.mean(scaled, axis=-1, keepdims=True)
        - standard * jnp.mean(scaled * standard, axis=-1, keepdims=True)
    ) * factor


def local(
    tokens_in,
    exit_layer,
    layer_index,
    segment_ids,
    grad_out,
    first_gain,
    first_bias,
    query_weight,
    query_bias,
    key_weight,
    value_weight,
    value_bias,
    out_weight,
    out_bias,
    second_gain,
    second_bias,
    up_weight,
    up_bias,
    down_weight,
    down_bias,
):
    T, N = lax.axis_size("ctx"), lax.axis_size("dp")
    me = lax.axis_index("ctx")
    n, D = tokens_in.shape[1], tokens_in.shape[2]
    r = first_gain.shape[0]
    f = up_bias.shape[0]
    S = T * n
    B = max(HEAD_DIM, r)
    A = D // (T * B)
    L = A * B
    x = tokens_in[0]
    g_out = grad_out[0]
    active = (exit_layer[0] > layer_index[0]).astype(F32)

    x_all = lax.all_gather(x, "ctx", axis=0, tiled=True)
    natural = r % HEAD_DIM == 0
    if natural:
        w_out = turn_gather_dp(out_weight)
    else:
        w_all = lax.all_gather(out_weight, ("dp", "ctx"), axis=0, tiled=True).reshape(A, T, B, D)
        w_out = lax.dynamic_index_in_dim(w_all, me, 1, keepdims=False).reshape(L, D)
    vectors = [first_gain, first_bias, query_bias, value_bias, out_bias, second_gain, second_bias, down_bias, up_bias]
    vectors = [v.reshape(1, -1) for v in vectors + [active.astype(BF16), segment_ids[0].astype(BF16)]]
    got = exchange_ctx(pack_columns([query_weight, key_weight, value_weight], [(A, B)] * 3, vectors))
    qkv_rows, small_got = unpack_to_rows(got, r, (3 * L,), (x_all, w_out))
    up_packed = pack_columns([up_weight], [(N, f)], [])
    w_qkv = gather_dp(qkv_rows)
    small_width = max(r, f)
    params = turn_gather_dp(small_got[:, :9, :small_width].reshape(T * 9, small_width)).reshape(N, T, 9, small_width)
    g_all, g_begun = gather_ctx(after(g_out, qkv_rows))
    g_all = g_all.reshape(S, D)

    feature = lambda i: params[:, :, i, :r].reshape(D).astype(F32)
    gain_one, bias_one, bias_query, bias_value, bias_out, gain_two, bias_two, bias_down = (
        feature(i) for i in range(8)
    )
    bias_up = lax.dynamic_index_in_dim(params[:, :, 8, :f], me, 1, keepdims=False).reshape(N * f).astype(F32)
    active_row = small_got[:, 9, :n].reshape(S)
    segs = small_got[:, 10, :n].reshape(S).astype(jnp.int32)
    seg_col, seg_row = segs.reshape(S, 1), segs.reshape(1, S)
    own_heads = lambda v: lax.dynamic_index_in_dim(v.reshape(A, T, B), me, 1, keepdims=False).reshape(L)
    bias_qkv = jnp.concatenate([own_heads(bias_query), jnp.zeros((L,), F32), own_heads(bias_value)])

    standard_one, _ = standardize(x_all.astype(F32))
    normed_one = after((standard_one * gain_one + bias_one).astype(BF16), g_all)
    qkv = (dot(normed_one, w_qkv) + bias_qkv).astype(BF16)
    w_down = gather_dp(after(down_weight, qkv))
    up_got = exchange_ctx([*up_packed[:-1], after(up_packed[-1], g_begun)])
    mixed, log_total = attention_forward(qkv, seg_col, seg_row, ())
    (up_rows,) = unpack_to_rows(up_got, r, (N * f,), (mixed,))
    w_up = gather_dp(up_rows)
    branch = add_over_chips(chip_sums(mixed, w_out, NN, (up_rows,)))[0] + bias_out
    inputs = x.astype(F32)
    active_own = active[:, None]
    middle = inputs + active_own * branch

    standard_two, factor_two = standardize(middle)
    normed_two = (standard_two * gain_two + bias_two).astype(BF16)
    normed_two_all = gather_ctx(after(normed_two, cost=0))[0].reshape(S, D)
    grad_ffn = (active_row[:, None] * g_all).astype(BF16)
    hidden, grad_pre, grad_up_sum = feed_forward(normed_two_all, grad_ffn, w_up, bias_up.reshape(1, N * f), w_down)
    sums_two = chip_sums(grad_pre, w_up, NT)
    grad_normed_two, begun_two = add_over_chips(sums_two)
    hidden = after(hidden, sums_two[0])
    grad_down_part = dot(hidden, grad_ffn, TN).astype(BF16)
    grad_down = scatter_dp(grad_down_part)
    grad_up_part = dot(after(normed_two_all, sums_two[0]), grad_pre, TN).astype(BF16)
    grad_up_mine = scatter_dp(grad_up_part)
    feed_sums = chip_sums(after(hidden, begun_two), w_down, NN)
    grad_res = g_out.astype(F32)
    grad_middle = grad_res + norm_back(grad_normed_two, gain_two, standard_two, factor_two)
    grad_branch = after((active_own * grad_middle).astype(BF16), cost=250)

    grad_branch_all = gather_ctx(grad_branch)[0].reshape(S, D)
    grad_heads = dot(grad_branch_all, w_out, NT).astype(BF16)
    grad_out_w = dot(mixed, grad_branch_all, TN)
    if natural:
        grad_out_w = scatter_dp(grad_out_w.astype(BF16))
    else:
        spread = jnp.zeros((A, T, B, D), F32)
        spread = lax.dynamic_update_index_in_dim(spread, grad_out_w.reshape(A, B, D), me, 1)
        grad_out_w = lax.psum_scatter(spread.reshape(D, D), ("dp", "ctx"), scatter_dimension=0, tiled=True)
    grad_qkv = attention_backward(
        qkv, grad_heads, log_total, mixed, seg_col, seg_row, (grad_down, grad_up_mine)
    )

    grad_qkv_part = dot(normed_one, grad_qkv, TN).astype(BF16)
    feed, _ = add_over_chips([after(item, grad_branch_all) for item in feed_sums[:-1]] + feed_sums[-1:], (grad_qkv,))
    sums_one = chip_sums(grad_qkv, w_qkv, NT, (grad_qkv_part, feed, grad_out_w))
    grad_normed_one, begun_one = add_over_chips(sums_one)
    grad_normed_one = after(grad_normed_one, cost=0)
    layer_out = (middle + active_own * (feed + bias_down)).astype(BF16)[None]
    standard_in, factor_in = standardize(inputs)
    grad_in = (grad_middle + norm_back(grad_normed_one, gain_one, standard_in, factor_in)).astype(BF16)[None]

    partial_one = dot(after(grad_qkv, begun_one), w_qkv, NT)
    grad_gain_one = jnp.sum(partial_one * standard_one, axis=0)
    grad_bias_one = jnp.sum(partial_one, axis=0)
    grad_gain_two = jnp.sum(grad_normed_two * standard_two, axis=0)
    grad_bias_two = jnp.sum(grad_normed_two, axis=0)
    ctx_index = lax.broadcasted_iota(jnp.int32, (1, T, 1), 1)
    spread_heads = lambda v: jnp.where(ctx_index == me, v.reshape(A, 1, B), 0.0).reshape(D)
    grad_bias_qkv = jnp.sum(grad_qkv.astype(F32), axis=0)
    grad_out_sum = jnp.sum(grad_branch.astype(F32), axis=0)
    grad_down_sum = jnp.sum((active_own * grad_res), axis=0)
    features = jnp.stack(
        [
            grad_gain_one,
            grad_bias_one,
            spread_heads(grad_bias_qkv[:L]),
            spread_heads(grad_bias_qkv[2 * L :]),
            grad_out_sum,
            grad_gain_two,
            grad_bias_two,
            grad_down_sum,
        ]
    )
    features = features.reshape(8, N, T, r).transpose(1, 2, 0, 3).reshape(N, T, 8 * r)
    units = jnp.where(
        lax.broadcasted_iota(jnp.int32, (1, T, 1), 1) == me, grad_up_sum.reshape(N, 1, f), 0.0
    )
    sums = jnp.concatenate([features, units], axis=2).reshape(N, T * (8 * r + f))
    sums = reduce_dp_small(sums).reshape(T, 8 * r + f)
    grad_qkv_mine = scatter_dp(grad_qkv_part)
    sums = sums.reshape(T, 8 + f // r, r).transpose(0, 2, 1)
    coarse = sums.astype(BF16)
    fine = (sums - coarse.astype(F32)).astype(BF16)
    more = jnp.pad(jnp.concatenate([coarse, fine], axis=2), ((0, 0), (0, 0), (0, 128 - 2 * sums.shape[2])))
    grad_got = exchange_ctx(pack_rows([after(grad_qkv_mine, grad_normed_one), grad_up_mine], more, r))
    grad_q, grad_k, grad_v, grad_up, *lines = unpack_to_columns(grad_got, [(A, B)] * 3 + [(N, f)], [r] * 8 + [f])
    shard = lambda i: lines[i].reshape(-1)
    return (
        layer_out,
        grad_in,
        shard(0),
        shard(1),
        grad_q,
        shard(2),
        grad_k,
        grad_v,
        shard(3),
        grad_out_w.astype(F32),
        shard(4),
        shard(5),
        shard(6),
        grad_up,
        shard(8),
        after(grad_down, grad_got[0]).astype(F32),
        shard(7),
    )


def solution(mesh):
    rows = P("dp", "ctx", None)
    flags = P("dp", "ctx")
    vector = P(("dp", "ctx"))
    matrix = P(("dp", "ctx"), None)
    in_specs = (
        rows, flags, P(), flags, rows, vector, vector, matrix, vector, matrix,
        matrix, vector, matrix, vector, vector, vector, matrix, vector, matrix, vector,
    )
    out_specs = (
        rows, rows, vector, vector, matrix, vector, matrix, matrix, vector, matrix,
        vector, vector, vector, matrix, vector, matrix, vector,
    )
    return jax.shard_map(local, mesh=mesh, in_specs=in_specs, out_specs=out_specs, check_vma=False)
```

```python
import jax
import jax.numpy as jnp
from jax import lax
from jax.experimental import pallas as pl
from jax.experimental.pallas import tpu as pltpu
from jax.sharding import PartitionSpec as P

HEADS = 32
HEAD_DIM = 64
EPSILON = 1e-05
NEG_FILL = -1e30
SCALE = HEAD_DIM ** (-0.5)
QUERY_BLOCK = 256
BF16 = jnp.bfloat16
F32 = jnp.float32

NN = (((1,), (0,)), ((), ()))
NT = (((1,), (1,)), ((), ()))
TN = (((0,), (0,)), ((), ()))
ANYWHERE = pl.BlockSpec(memory_space=pl.ANY)


def dot(left, right, dims=NN):
    return lax.dot_general(left, right, dims, preferred_element_type=F32)


def forward_kernel(*refs, heads, lanes, block):
    qkv_ref, seg_col_ref, seg_row_ref = refs[:3]
    mixed_ref, log_ref = refs[-2:]
    rows = qkv_ref.shape[0]
    head_of_lane = lax.broadcasted_iota(jnp.int32, (1, lanes), 1) // HEAD_DIM
    diagonal = lax.broadcasted_iota(jnp.int32, (block, block), 1) <= lax.broadcasted_iota(
        jnp.int32, (block, block), 0
    )
    for b in range(rows // block):
        low, high = b * block, (b + 1) * block
        queries = qkv_ref[low:high, :lanes] * jnp.asarray(SCALE, BF16)
        keys = qkv_ref[:high, lanes : 2 * lanes]
        values = qkv_ref[:high, 2 * lanes :]
        allowed = seg_col_ref[low:high, :] == seg_row_ref[:, :high]
        last = allowed[:, low:] & diagonal
        allowed = jnp.concatenate([allowed[:, :low], last], axis=1) if b else last
        mixed = jnp.zeros((block, lanes), F32)
        for h in range(heads):
            mine = head_of_lane == h
            scores = dot(jnp.where(mine, queries, jnp.zeros_like(queries)), keys, NT)
            scores = jnp.where(allowed, scores, NEG_FILL)
            top = jnp.max(scores, axis=1, keepdims=True)
            weights = jnp.exp(scores - top)
            total = jnp.sum(weights, axis=1, keepdims=True)
            product = dot(weights.astype(BF16), values)
            mixed = mixed + jnp.where(mine, product / total, 0.0)
            log_total = jnp.broadcast_to(top + jnp.log(total), (block, 128))
            log_ref[h : h + 1, low:high] = jnp.transpose(log_total)[:1, :]
        mixed_ref[low:high, :] = mixed.astype(BF16)


def backward_kernel(*refs, heads, lanes, block):
    qkv_ref, grad_ref, log_ref, mixed_ref, seg_col_ref, seg_row_ref = refs[:6]
    out_ref, dk_ref, dv_ref = refs[-3:]
    rows = qkv_ref.shape[0]
    head_of_lane = lax.broadcasted_iota(jnp.int32, (1, lanes), 1) // HEAD_DIM
    diagonal = lax.broadcasted_iota(jnp.int32, (block, block), 0) <= lax.broadcasted_iota(
        jnp.int32, (block, block), 1
    )
    scale = jnp.asarray(SCALE, BF16)
    head_rows = jnp.where(lax.broadcasted_iota(jnp.int32, (16, lanes), 0) == head_of_lane, 1.0, 0.0).astype(BF16)
    for b in range(rows // block):
        low, high = b * block, (b + 1) * block
        queries = qkv_ref[low:high, :lanes] * scale
        grads = grad_ref[low:high, :]
        keys = qkv_ref[:high, lanes : 2 * lanes]
        values = qkv_ref[:high, 2 * lanes :]
        allowed = seg_col_ref[:high, :] == seg_row_ref[:, low:high]
        last = allowed[low:, :] & diagonal
        allowed = jnp.concatenate([allowed[:low, :], last], axis=0) if b else last
        products = grads.astype(F32) * mixed_ref[low:high, :].astype(F32)
        coarse = products.astype(BF16)
        fine = (products - coarse.astype(F32)).astype(BF16)
        delta = dot(head_rows, coarse, NT) + dot(head_rows, fine, NT)
        grad_queries = jnp.zeros((block, lanes), F32)
        grad_keys = jnp.zeros((high, lanes), F32)
        grad_values = jnp.zeros((high, lanes), F32)
        for h in range(heads):
            mine = head_of_lane == h
            query_h = jnp.where(mine, queries, jnp.zeros_like(queries))
            grad_h = jnp.where(mine, grads, jnp.zeros_like(grads))
            scores = dot(keys, query_h, NT)
            probs = jnp.where(allowed, jnp.exp(scores - log_ref[h : h + 1, low:high]), 0.0)
            grad_probs = dot(values, grad_h, NT)
            grad_scores = (probs * (grad_probs - delta[h : h + 1, :])).astype(BF16)
            grad_values = grad_values + dot(probs.astype(BF16), grad_h)
            grad_keys = grad_keys + dot(grad_scores, query_h)
            grad_queries = grad_queries + jnp.where(mine, dot(grad_scores, keys, TN), 0.0)
        out_ref[low:high, :lanes] = (grad_queries * SCALE).astype(BF16)
        if b:
            dk_ref[:low, :] = dk_ref[:low, :] + grad_keys[:low, :]
            dv_ref[:low, :] = dv_ref[:low, :] + grad_values[:low, :]
        dk_ref[low:high, :] = grad_keys[low:, :]
        dv_ref[low:high, :] = grad_values[low:, :]
    out_ref[:, lanes : 2 * lanes] = dk_ref[...].astype(BF16)
    out_ref[:, 2 * lanes :] = dv_ref[...].astype(BF16)


def attention_forward(qkv, seg_col, seg_row, earlier):
    rows, lanes = qkv.shape[0], qkv.shape[1] // 3
    heads = lanes // HEAD_DIM
    pairs = rows * rows * heads // 2
    return pl.pallas_call(
        lambda *refs: forward_kernel(*refs, heads=heads, lanes=lanes, block=QUERY_BLOCK),
        out_shape=(jax.ShapeDtypeStruct((rows, lanes), BF16), jax.ShapeDtypeStruct((heads, rows), F32)),
        compiler_params=pltpu.CompilerParams(vmem_limit_bytes=48 * 2**20),
        cost_estimate=pl.CostEstimate(flops=pairs * 5000, bytes_accessed=8 * rows * lanes, transcendentals=pairs),
        in_specs=[pl.BlockSpec(memory_space=pltpu.VMEM)] * 3 + [ANYWHERE] * len(earlier),
        name="attention_forward",
    )(qkv, seg_col, seg_row, *earlier)


def attention_backward(qkv, grads, log_total, mixed, seg_col, seg_row, earlier):
    rows, lanes = qkv.shape[0], qkv.shape[1] // 3
    heads = lanes // HEAD_DIM
    pairs = rows * rows * heads // 2
    return pl.pallas_call(
        lambda *refs: backward_kernel(*refs, heads=heads, lanes=lanes, block=QUERY_BLOCK),
        out_shape=jax.ShapeDtypeStruct((rows, 3 * lanes), BF16),
        scratch_shapes=[pltpu.VMEM((rows, lanes), F32), pltpu.VMEM((rows, lanes), F32)],
        compiler_params=pltpu.CompilerParams(vmem_limit_bytes=48 * 2**20),
        cost_estimate=pl.CostEstimate(flops=pairs * 5000, bytes_accessed=14 * rows * lanes, transcendentals=pairs),
        in_specs=[pl.BlockSpec(memory_space=pltpu.VMEM)] * 6 + [ANYWHERE] * len(earlier),
        name="attention_backward",
    )(qkv, grads, log_total, mixed, seg_col, seg_row, *earlier)


def feed_kernel(normed_ref, grad_ref, up_ref, bias_ref, down_ref, hidden_ref, pre_ref, sum_ref):
    block = 2 * QUERY_BLOCK
    total = jnp.zeros(sum_ref.shape, F32)
    down = jnp.transpose(down_ref[...])
    for low in range(0, normed_ref.shape[0], block):
        rows = slice(low, low + block)
        u = dot(normed_ref[rows, :], up_ref[...]) + bias_ref[...]
        grad_hidden = dot(grad_ref[rows, :], down)
        square = u * u
        bend = jnp.tanh(u * (0.7978845608028654 + (0.7978845608028654 * 0.044715) * square))
        half = 0.5 + 0.5 * bend
        hidden_ref[rows, :] = (u * half).astype(BF16)
        slope = half + u * (half * (1.0 - bend)) * (
            0.7978845608028654 + (3.0 * 0.7978845608028654 * 0.044715) * square
        )
        grad_pre = (grad_hidden * slope).astype(BF16)
        pre_ref[rows, :] = grad_pre
        total = total + jnp.sum(grad_pre.astype(F32), axis=0, keepdims=True)
    sum_ref[...] = total


def feed_forward(normed, grad, w_up, bias, w_down):
    rows, width = normed.shape
    units = w_up.shape[1]
    tile = min(units, 256)
    whole = pl.BlockSpec((rows, width), lambda i: (0, 0))
    column = pl.BlockSpec((rows, tile), lambda i: (0, i))
    line = pl.BlockSpec((1, tile), lambda i: (0, i))
    return pl.pallas_call(
        feed_kernel,
        grid=(units // tile,),
        out_shape=(
            jax.ShapeDtypeStruct((rows, units), BF16),
            jax.ShapeDtypeStruct((rows, units), BF16),
            jax.ShapeDtypeStruct((1, units), F32),
        ),
        in_specs=[
            whole,
            whole,
            pl.BlockSpec((width, tile), lambda i: (0, i)),
            line,
            pl.BlockSpec((tile, width), lambda i: (i, 0)),
        ],
        out_specs=(column, column, line),
        compiler_params=pltpu.CompilerParams(vmem_limit_bytes=56 * 2**20),
        cost_estimate=pl.CostEstimate(
            flops=4 * rows * width * units, bytes_accessed=4 * rows * width, transcendentals=rows * units
        ),
        name="feed_forward",
    )(normed, grad, w_up, bias, w_down)


def chips():
    return lax.axis_size("ctx") // 2


def turn(value, k):
    count = chips()
    return lax.ppermute(
        value, "ctx", [(2 * s + core, 2 * ((s + k) % count) + core) for s in range(count) for core in range(2)]
    )


FAR = ((0, 2), (1, 3), (2, 0), (3, 1))
NEAR = ((0, 1), (1, 0), (2, 3), (3, 2))
MIDDLE = ((1, 2), (2, 1))
OUT = ((2, 3), (1, 0))
BACK = ((3, 2), (0, 1))


def chip_permute(value, pairs):
    return lax.ppermute(value, "ctx", [(2 * s + core, 2 * t + core) for s, t in pairs for core in range(2)])


def swap(value):
    return lax.ppermute(value, "ctx", [(i, i ^ 1) for i in range(2 * chips())])


def place():
    me = lax.axis_index("ctx")
    return me // 2, me % 2


def after(value, *earlier, cost=0):
    def nothing(*refs):
        pass

    return pl.pallas_call(
        nothing,
        out_shape=jax.ShapeDtypeStruct(value.shape, value.dtype),
        in_specs=[ANYWHERE] * (1 + len(earlier)),
        out_specs=ANYWHERE,
        input_output_aliases={0: 0},
        cost_estimate=pl.CostEstimate(flops=cost * 10**9, bytes_accessed=cost * 3 * 10**6, transcendentals=0),
        name="after",
    )(value, *earlier)


def gather_ctx(block, relay=False):
    count = chips()
    chip, core = place()
    if relay and count == 4:
        far, near, middle = (chip_permute(block, pairs) for pairs in (FAR, NEAR, MIDDLE))
        last = jnp.where((chip == 0) | (chip == 3), chip_permute(far, OUT), middle)
        same, chip_of = [block, near, far, last], [chip, chip ^ 1, chip ^ 2, chip ^ 3]
    else:
        same = [block] + [turn(block, k) for k in range(1, count)]
        chip_of = [(chip + count - k) % count for k in range(count)]
    other = [swap(item) for item in same]
    out = jnp.zeros((2 * count,) + block.shape, block.dtype)
    for k in range(count):
        base = 2 * chip_of[k]
        out = lax.dynamic_update_index_in_dim(out, same[k], base + core, 0)
        out = lax.dynamic_update_index_in_dim(out, other[k], base + 1 - core, 0)
    return out, same[1]


def where_am_i():
    return jnp.stack(place()).astype(jnp.int32)


def pack_columns(weights, cuts, vectors):
    count = chips()
    r = weights[0].shape[0]
    total = sum(lead * width for lead, width in cuts)
    below = -(-len(vectors) // 16) * 16

    def kernel(at_ref, *refs):
        ins, outs = refs[: len(weights)], refs[-(count + 1) :]
        chip, core = at_ref[0], at_ref[1]
        for j in range(2 * count):
            pieces = [
                ref[:, (a * 2 * count + j) * width : (a * 2 * count + j + 1) * width]
                for ref, (lead, width) in zip(ins, cuts)
                for a in range(lead)
            ]
            block = jnp.concatenate(pieces, axis=1)
            slot = lax.rem(j // 2 + count - chip, count)
            for k in range(count):

                @pl.when((slot == k) & (core == j % 2))
                def _(k=k, block=block):
                    outs[k][:r, :] = block

                @pl.when((slot == k) & (core != j % 2))
                def _(k=k, block=block):
                    outs[count][k, :r, :] = block

        if vectors:
            lines = [ref[...].astype(F32) for ref in refs[len(weights) : len(weights) + len(vectors)]]
            lines = [
                jnp.concatenate([line, jnp.zeros((1, total - line.shape[1]), F32)], axis=1) for line in lines
            ]
            more = jnp.concatenate(lines + [jnp.zeros((below - len(lines), total), F32)], axis=0).astype(BF16)
            for k in range(count):
                outs[k][r:, :] = more
                outs[count][k, r:, :] = more

    block_shape = jax.ShapeDtypeStruct((r + below, total), BF16)
    return pl.pallas_call(
        kernel,
        out_shape=[block_shape] * count + [jax.ShapeDtypeStruct((count,) + block_shape.shape, BF16)],
        in_specs=[pl.BlockSpec(memory_space=pltpu.SMEM)]
        + [pl.BlockSpec(memory_space=pltpu.VMEM)] * (len(weights) + len(vectors)),
        name="pack_columns",
    )(where_am_i(), *weights, *vectors)


def pack_rows(arrays, more, height):
    count = chips()
    width = sum(item.shape[1] for item in arrays)
    total = width + more.shape[2]

    def kernel(at_ref, *refs):
        ins, outs = refs[: len(arrays)], refs[-(count + 1) :]
        chip, core = at_ref[0], at_ref[1]
        for k in range(count):
            base = 2 * lax.rem(chip + k, count)
            start = 0
            for ref in ins:
                end = start + ref.shape[1]
                mine = pl.ds(pl.multiple_of((base + core) * height, height), height)
                other = pl.ds(pl.multiple_of((base + 1 - core) * height, height), height)
                outs[k][:, start:end] = ref[mine, :]
                outs[count][k, :, start:end] = ref[other, :]
                start = end
            outs[k][:, width:] = refs[len(arrays)][base + core]
            outs[count][k, :, width:] = refs[len(arrays)][base + 1 - core]

    block_shape = jax.ShapeDtypeStruct((height, total), BF16)
    return pl.pallas_call(
        kernel,
        out_shape=[block_shape] * count + [jax.ShapeDtypeStruct((count,) + block_shape.shape, BF16)],
        in_specs=[pl.BlockSpec(memory_space=pltpu.SMEM)] + [pl.BlockSpec(memory_space=pltpu.VMEM)] * (1 + len(arrays)),
        name="pack_rows",
    )(where_am_i(), *arrays, more)


def exchange_ctx(packed):
    count = chips()
    arrived = swap(packed[count])
    both = [jnp.stack([packed[k], arrived[k]]) for k in range(count)]
    return [both[0]] + [turn(both[k], k) for k in range(1, count)]


def source_index(at_ref, k, side, count):
    core = at_ref[1] if side == 0 else 1 - at_ref[1]
    return 2 * lax.rem(at_ref[0] + count - k, count) + core


def unpack_to_rows(got, r, widths, earlier):
    count = chips()
    height, total = got[0].shape[1:]
    below = height - r

    def kernel(at_ref, *refs):
        ins, outs = refs[:count], refs[count + len(earlier) :]
        for k in range(count):
            for side in range(2):
                index = source_index(at_ref, k, side, count)
                start = 0
                for out, width in zip(outs, widths):
                    out[pl.ds(pl.multiple_of(index * r, r), r), :] = ins[k][side, :r, start : start + width]
                    start += width
                if below:
                    outs[-1][index] = ins[k][side, r:, :]

    return pl.pallas_call(
        kernel,
        out_shape=[jax.ShapeDtypeStruct((2 * count * r, width), BF16) for width in widths]
        + [jax.ShapeDtypeStruct((2 * count, below, total), BF16)] * (below > 0),
        in_specs=[pl.BlockSpec(memory_space=pltpu.SMEM)]
        + [pl.BlockSpec(memory_space=pltpu.VMEM)] * count
        + [ANYWHERE] * len(earlier),
        name="unpack_to_rows",
    )(where_am_i(), *got, *earlier)


def unpack_to_columns(got, cuts, lengths):
    count = chips()
    r, total = got[0].shape[1:]

    def kernel(at_ref, *refs):
        ins, outs, held = refs[:count], refs[count:-1], refs[-1]
        for k in range(count):
            for side in range(2):
                held[source_index(at_ref, k, side, count)] = ins[k][side]
        for j in range(2 * count):
            block = held[j].astype(F32)
            start = 0
            for out, (lead, width) in zip(outs, cuts):
                for a in range(lead):
                    column = (a * 2 * count + j) * width
                    out[:, column : column + width] = block[:, start : start + width]
                    start += width
        added = held[0, :, total - 128 :].astype(F32)
        for j in range(1, 2 * count):
            added = added + held[j, :, total - 128 :].astype(F32)
        lines = jnp.transpose(added)
        columns = sum(lengths) // r
        at = 0
        for out, length in zip(outs[len(cuts) :], lengths):
            parts = [
                lines[i : i + 1, :] + lines[columns + i : columns + i + 1, :] for i in range(at, at + length // r)
            ]
            out[...] = parts[0] if len(parts) == 1 else jnp.concatenate(parts, axis=1)
            at += length // r

    return pl.pallas_call(
        kernel,
        out_shape=[jax.ShapeDtypeStruct((r, 2 * count * lead * width), F32) for lead, width in cuts]
        + [jax.ShapeDtypeStruct((1, length), F32) for length in lengths],
        in_specs=[pl.BlockSpec(memory_space=pltpu.SMEM)] + [pl.BlockSpec(memory_space=pltpu.VMEM)] * count,
        scratch_shapes=[pltpu.VMEM((2 * count, r, total), BF16)],
        name="unpack_to_columns",
    )(where_am_i(), *got)


def split_rows(rows, relay):
    count = chips()
    chip, core = place()
    pairs = rows.reshape((count, 2, rows.shape[0] // (2 * count), rows.shape[1]))
    order = [chip ^ (3 - k) for k in range(4)] if relay and count == 4 else [(chip + k) % count for k in range(1, count + 1)]
    turned = [lax.dynamic_index_in_dim(pairs, index, 0, keepdims=False) for index in order]
    pick = lambda which: jnp.concatenate(
        [lax.dynamic_index_in_dim(item, which, 0, keepdims=False) for item in turned], axis=0
    )
    return pick(core), pick(1 - core)


def chip_sums(left, right, dims, earlier=(), relay=False):
    count = chips()
    mine, other = split_rows(left, relay)
    leaving = dot(other, right, dims).astype(BF16)
    arrived = swap(after(leaving, *earlier) if earlier else leaving)
    own = dot(mine, right, dims)
    n = own.shape[0] // count
    sums = [own[k * n : (k + 1) * n] + arrived[k * n : (k + 1) * n].astype(F32) for k in range(count)]
    return [item.astype(BF16) for item in sums[:-1]] + sums[-1:]


def add_over_chips(sums, earlier=(), relay=False):
    count = chips()
    total = sums[-1]
    if relay and count == 4:
        ends, middle, near = (chip_permute(*pair) for pair in ((sums[0], BACK), (sums[0], MIDDLE), (sums[2], NEAR)))
        far = chip_permute((sums[1].astype(F32) + ends.astype(F32)).astype(BF16), FAR)
        for arrived in (middle, near, far):
            arrived = after(arrived, *earlier) if earlier else arrived
            total = total + arrived.astype(F32)
        return total, near
    for k in range(1, count):
        arrived = turn(sums[k - 1], k)
        arrived = after(arrived, *earlier) if earlier else arrived
        total = total + arrived.astype(F32)
        first = arrived if k == 1 else first
    return total, first


def reduce_dp_small(blocks):
    parts = lax.axis_size("dp")
    me = lax.axis_index("dp")
    total = lax.dynamic_index_in_dim(blocks, me, 0, keepdims=False)
    for k in range(1, parts):
        piece = lax.dynamic_index_in_dim(blocks, (me + k) % parts, 0, keepdims=False)
        total = total + lax.ppermute(piece, "dp", [(i, (i + k) % parts) for i in range(parts)])
    return total


def gather_dp(value):
    return lax.all_gather(value, "dp", axis=0, tiled=True)


def scatter_dp(value):
    return lax.psum_scatter(value, "dp", scatter_dimension=0, tiled=True)


def across(value, k):
    return lax.ppermute(value, "dp", [(i, i ^ k) for i in range(lax.axis_size("dp"))])


def turn_gather_dp(value):
    parts = lax.axis_size("dp")
    me = lax.axis_index("dp")
    out = jnp.zeros((parts,) + value.shape, value.dtype)
    out = lax.dynamic_update_index_in_dim(out, value, me, 0)
    for k in range(1, parts):
        out = lax.dynamic_update_index_in_dim(out, across(value, k), me ^ k, 0)
    return out.reshape((parts * value.shape[0],) + value.shape[1:])


def turn_scatter_dp(blocks):
    parts = lax.axis_size("dp")
    me = lax.axis_index("dp")
    blocks = blocks.reshape((parts, blocks.shape[0] // parts) + blocks.shape[1:])
    total = lax.dynamic_index_in_dim(blocks, me, 0, keepdims=False).astype(F32)
    for k in range(1, parts):
        total = total + across(lax.dynamic_index_in_dim(blocks, me ^ k, 0, keepdims=False), k).astype(F32)
    return total


def standardize(values):
    average = jnp.mean(values, axis=-1, keepdims=True)
    centered = values - average
    variance = jnp.mean(centered * centered, axis=-1, keepdims=True)
    factor = lax.rsqrt(variance + EPSILON)
    return centered * factor, factor


def norm_back(grad, gain, standard, factor):
    scaled = grad * gain
    return (
        scaled
        - jnp.mean(scaled, axis=-1, keepdims=True)
        - standard * jnp.mean(scaled * standard, axis=-1, keepdims=True)
    ) * factor


def local(
    tokens_in,
    exit_layer,
    layer_index,
    segment_ids,
    grad_out,
    first_gain,
    first_bias,
    query_weight,
    query_bias,
    key_weight,
    value_weight,
    value_bias,
    out_weight,
    out_bias,
    second_gain,
    second_bias,
    up_weight,
    up_bias,
    down_weight,
    down_bias,
):
    T, N = lax.axis_size("ctx"), lax.axis_size("dp")
    me = lax.axis_index("ctx")
    n, D = tokens_in.shape[1], tokens_in.shape[2]
    r = first_gain.shape[0]
    f = up_bias.shape[0]
    S = T * n
    B = max(HEAD_DIM, r)
    A = D // (T * B)
    L = A * B
    x = tokens_in[0]
    g_out = grad_out[0]
    active = (exit_layer[0] > layer_index[0]).astype(F32)

    x_all = lax.all_gather(x, "ctx", axis=0, tiled=True)
    natural = r % HEAD_DIM == 0
    if natural:
        w_out = turn_gather_dp(out_weight)
    else:
        w_all = lax.all_gather(out_weight, ("dp", "ctx"), axis=0, tiled=True).reshape(A, T, B, D)
        w_out = lax.dynamic_index_in_dim(w_all, me, 1, keepdims=False).reshape(L, D)
    vectors = [first_gain, first_bias, query_bias, value_bias, out_bias, second_gain, second_bias, down_bias, up_bias]
    vectors = [v.reshape(1, -1) for v in vectors + [active.astype(BF16), segment_ids[0].astype(BF16)]]
    got = exchange_ctx(pack_columns([query_weight, key_weight, value_weight], [(A, B)] * 3, vectors))
    qkv_rows, small_got = unpack_to_rows(got, r, (3 * L,), (x_all, w_out))
    up_packed = pack_columns([up_weight], [(N, f)], [])
    w_qkv = gather_dp(qkv_rows)
    small_width = max(r, f)
    params = turn_gather_dp(small_got[:, :9, :small_width].reshape(T * 9, small_width)).reshape(N, T, 9, small_width)
    g_all, g_begun = gather_ctx(after(g_out, qkv_rows))
    g_all = g_all.reshape(S, D)

    feature = lambda i: params[:, :, i, :r].reshape(D).astype(F32)
    gain_one, bias_one, bias_query, bias_value, bias_out, gain_two, bias_two, bias_down = (
        feature(i) for i in range(8)
    )
    bias_up = lax.dynamic_index_in_dim(params[:, :, 8, :f], me, 1, keepdims=False).reshape(N * f).astype(F32)
    active_row = small_got[:, 9, :n].reshape(S)
    segs = small_got[:, 10, :n].reshape(S).astype(jnp.int32)
    seg_col, seg_row = segs.reshape(S, 1), segs.reshape(1, S)
    own_heads = lambda v: lax.dynamic_index_in_dim(v.reshape(A, T, B), me, 1, keepdims=False).reshape(L)
    bias_qkv = jnp.concatenate([own_heads(bias_query), jnp.zeros((L,), F32), own_heads(bias_value)])

    standard_one, _ = standardize(x_all.astype(F32))
    normed_one = after((standard_one * gain_one + bias_one).astype(BF16), g_all)
    qkv = (dot(normed_one, w_qkv) + bias_qkv).astype(BF16)
    w_down = gather_dp(after(down_weight, qkv))
    up_got = exchange_ctx([*up_packed[:-1], after(up_packed[-1], g_begun)])
    mixed, log_total = attention_forward(qkv, seg_col, seg_row, ())
    (up_rows,) = unpack_to_rows(up_got, r, (N * f,), (mixed,))
    w_up = gather_dp(up_rows)
    branch = add_over_chips(chip_sums(mixed, w_out, NN, (up_rows,), True), relay=True)[0] + bias_out
    inputs = x.astype(F32)
    active_own = active[:, None]
    middle = inputs + active_own * branch

    standard_two, factor_two = standardize(middle)
    normed_two = (standard_two * gain_two + bias_two).astype(BF16)
    normed_two_all = gather_ctx(after(normed_two, cost=0), True)[0].reshape(S, D)
    grad_ffn = (active_row[:, None] * g_all).astype(BF16)
    hidden, grad_pre, grad_up_sum = feed_forward(normed_two_all, grad_ffn, w_up, bias_up.reshape(1, N * f), w_down)
    sums_two = chip_sums(grad_pre, w_up, NT)
    grad_normed_two, begun_two = add_over_chips(sums_two)
    hidden = after(hidden, sums_two[0])
    grad_down_part = dot(hidden, grad_ffn, TN).astype(BF16)
    grad_down = scatter_dp(grad_down_part)
    grad_up_part = dot(after(normed_two_all, sums_two[0]), grad_pre, TN).astype(BF16)
    grad_up_mine = scatter_dp(grad_up_part)
    feed_sums = chip_sums(after(hidden, begun_two), w_down, NN)
    grad_res = g_out.astype(F32)
    grad_middle = grad_res + norm_back(grad_normed_two, gain_two, standard_two, factor_two)
    grad_branch = after((active_own * grad_middle).astype(BF16), cost=250)

    grad_branch_all = gather_ctx(grad_branch)[0].reshape(S, D)
    grad_heads = dot(grad_branch_all, w_out, NT).astype(BF16)
    grad_out_w = dot(mixed, grad_branch_all, TN)
    if natural:
        grad_out_w = scatter_dp(grad_out_w.astype(BF16))
    else:
        spread = jnp.zeros((A, T, B, D), F32)
        spread = lax.dynamic_update_index_in_dim(spread, grad_out_w.reshape(A, B, D), me, 1)
        grad_out_w = lax.psum_scatter(spread.reshape(D, D), ("dp", "ctx"), scatter_dimension=0, tiled=True)
    grad_qkv = attention_backward(
        qkv, grad_heads, log_total, mixed, seg_col, seg_row, (grad_down, grad_up_mine)
    )

    grad_qkv_part = dot(normed_one, grad_qkv, TN).astype(BF16)
    feed, _ = add_over_chips([after(item, grad_branch_all) for item in feed_sums[:-1]] + feed_sums[-1:], (grad_qkv,))
    sums_one = chip_sums(grad_qkv, w_qkv, NT, (grad_qkv_part, feed, grad_out_w))
    grad_normed_one, begun_one = add_over_chips(sums_one)
    grad_normed_one = after(grad_normed_one, cost=0)
    layer_out = (middle + active_own * (feed + bias_down)).astype(BF16)[None]
    standard_in, factor_in = standardize(inputs)
    grad_in = (grad_middle + norm_back(grad_normed_one, gain_one, standard_in, factor_in)).astype(BF16)[None]

    partial_one = dot(after(grad_qkv, begun_one), w_qkv, NT)
    grad_gain_one = jnp.sum(partial_one * standard_one, axis=0)
    grad_bias_one = jnp.sum(partial_one, axis=0)
    grad_gain_two = jnp.sum(grad_normed_two * standard_two, axis=0)
    grad_bias_two = jnp.sum(grad_normed_two, axis=0)
    ctx_index = lax.broadcasted_iota(jnp.int32, (1, T, 1), 1)
    spread_heads = lambda v: jnp.where(ctx_index == me, v.reshape(A, 1, B), 0.0).reshape(D)
    grad_bias_qkv = jnp.sum(grad_qkv.astype(F32), axis=0)
    grad_out_sum = jnp.sum(grad_branch.astype(F32), axis=0)
    grad_down_sum = jnp.sum((active_own * grad_res), axis=0)
    features = jnp.stack(
        [
            grad_gain_one,
            grad_bias_one,
            spread_heads(grad_bias_qkv[:L]),
            spread_heads(grad_bias_qkv[2 * L :]),
            grad_out_sum,
            grad_gain_two,
            grad_bias_two,
            grad_down_sum,
        ]
    )
    features = features.reshape(8, N, T, r).transpose(1, 2, 0, 3).reshape(N, T, 8 * r)
    units = jnp.where(
        lax.broadcasted_iota(jnp.int32, (1, T, 1), 1) == me, grad_up_sum.reshape(N, 1, f), 0.0
    )
    sums = jnp.concatenate([features, units], axis=2).reshape(N, T * (8 * r + f))
    sums = reduce_dp_small(sums).reshape(T, 8 * r + f)
    grad_qkv_mine = scatter_dp(grad_qkv_part)
    sums = sums.reshape(T, 8 + f // r, r).transpose(0, 2, 1)
    coarse = sums.astype(BF16)
    fine = (sums - coarse.astype(F32)).astype(BF16)
    more = jnp.pad(jnp.concatenate([coarse, fine], axis=2), ((0, 0), (0, 0), (0, 128 - 2 * sums.shape[2])))
    grad_got = exchange_ctx(pack_rows([after(grad_qkv_mine, grad_normed_one), grad_up_mine], more, r))
    grad_q, grad_k, grad_v, grad_up, *lines = unpack_to_columns(grad_got, [(A, B)] * 3 + [(N, f)], [r] * 8 + [f])
    shard = lambda i: lines[i].reshape(-1)
    return (
        layer_out,
        grad_in,
        shard(0),
        shard(1),
        grad_q,
        shard(2),
        grad_k,
        grad_v,
        shard(3),
        grad_out_w.astype(F32),
        shard(4),
        shard(5),
        shard(6),
        grad_up,
        shard(8),
        after(grad_down, grad_got[0]).astype(F32),
        shard(7),
    )


def solution(mesh):
    rows = P("dp", "ctx", None)
    flags = P("dp", "ctx")
    vector = P(("dp", "ctx"))
    matrix = P(("dp", "ctx"), None)
    in_specs = (
        rows, flags, P(), flags, rows, vector, vector, matrix, vector, matrix,
        matrix, vector, matrix, vector, vector, vector, matrix, vector, matrix, vector,
    )
    out_specs = (
        rows, rows, vector, vector, matrix, vector, matrix, matrix, vector, matrix,
        vector, vector, vector, matrix, vector, matrix, vector,
    )
    return jax.shard_map(local, mesh=mesh, in_specs=in_specs, out_specs=out_specs, check_vma=False)
```

```python
import jax
import jax.numpy as jnp
from jax import lax
from jax.experimental import pallas as pl
from jax.experimental.pallas import tpu as pltpu
from jax.sharding import PartitionSpec as P

HEADS = 32
HEAD_DIM = 64
EPSILON = 1e-05
NEG_FILL = -1e30
SCALE = HEAD_DIM ** (-0.5)
QUERY_BLOCK = 256
BF16 = jnp.bfloat16
F32 = jnp.float32

NN = (((1,), (0,)), ((), ()))
NT = (((1,), (1,)), ((), ()))
TN = (((0,), (0,)), ((), ()))
ANYWHERE = pl.BlockSpec(memory_space=pl.ANY)


def dot(left, right, dims=NN):
    return lax.dot_general(left, right, dims, preferred_element_type=F32)


def forward_kernel(*refs, heads, lanes, block):
    qkv_ref, seg_col_ref, seg_row_ref = refs[:3]
    mixed_ref, log_ref = refs[-2:]
    rows = qkv_ref.shape[0]
    head_of_lane = lax.broadcasted_iota(jnp.int32, (1, lanes), 1) // HEAD_DIM
    diagonal = lax.broadcasted_iota(jnp.int32, (block, block), 1) <= lax.broadcasted_iota(
        jnp.int32, (block, block), 0
    )
    for b in range(rows // block):
        low, high = b * block, (b + 1) * block
        queries = qkv_ref[low:high, :lanes] * jnp.asarray(SCALE, BF16)
        keys = qkv_ref[:high, lanes : 2 * lanes]
        values = qkv_ref[:high, 2 * lanes :]
        allowed = seg_col_ref[low:high, :] == seg_row_ref[:, :high]
        last = allowed[:, low:] & diagonal
        allowed = jnp.concatenate([allowed[:, :low], last], axis=1) if b else last
        mixed = jnp.zeros((block, lanes), F32)
        for h in range(heads):
            mine = head_of_lane == h
            scores = dot(jnp.where(mine, queries, jnp.zeros_like(queries)), keys, NT)
            scores = jnp.where(allowed, scores, NEG_FILL)
            top = jnp.max(scores, axis=1, keepdims=True)
            weights = jnp.exp(scores - top)
            total = jnp.sum(weights, axis=1, keepdims=True)
            product = dot(weights.astype(BF16), values)
            mixed = mixed + jnp.where(mine, product / total, 0.0)
            log_total = jnp.broadcast_to(top + jnp.log(total), (block, 128))
            log_ref[h : h + 1, low:high] = jnp.transpose(log_total)[:1, :]
        mixed_ref[low:high, :] = mixed.astype(BF16)


def backward_kernel(*refs, heads, lanes, block):
    qkv_ref, grad_ref, log_ref, mixed_ref, seg_col_ref, seg_row_ref = refs[:6]
    out_ref, dk_ref, dv_ref = refs[-3:]
    rows = qkv_ref.shape[0]
    head_of_lane = lax.broadcasted_iota(jnp.int32, (1, lanes), 1) // HEAD_DIM
    diagonal = lax.broadcasted_iota(jnp.int32, (block, block), 0) <= lax.broadcasted_iota(
        jnp.int32, (block, block), 1
    )
    scale = jnp.asarray(SCALE, BF16)
    head_rows = jnp.where(lax.broadcasted_iota(jnp.int32, (16, lanes), 0) == head_of_lane, 1.0, 0.0).astype(BF16)
    for b in range(rows // block):
        low, high = b * block, (b + 1) * block
        queries = qkv_ref[low:high, :lanes] * scale
        grads = grad_ref[low:high, :]
        keys = qkv_ref[:high, lanes : 2 * lanes]
        values = qkv_ref[:high, 2 * lanes :]
        allowed = seg_col_ref[:high, :] == seg_row_ref[:, low:high]
        last = allowed[low:, :] & diagonal
        allowed = jnp.concatenate([allowed[:low, :], last], axis=0) if b else last
        products = grads.astype(F32) * mixed_ref[low:high, :].astype(F32)
        coarse = products.astype(BF16)
        fine = (products - coarse.astype(F32)).astype(BF16)
        delta = dot(head_rows, coarse, NT) + dot(head_rows, fine, NT)
        grad_queries = jnp.zeros((block, lanes), F32)
        grad_keys = jnp.zeros((high, lanes), F32)
        grad_values = jnp.zeros((high, lanes), F32)
        for h in range(heads):
            mine = head_of_lane == h
            query_h = jnp.where(mine, queries, jnp.zeros_like(queries))
            grad_h = jnp.where(mine, grads, jnp.zeros_like(grads))
            scores = dot(keys, query_h, NT)
            probs = jnp.where(allowed, jnp.exp(scores - log_ref[h : h + 1, low:high]), 0.0)
            grad_probs = dot(values, grad_h, NT)
            grad_scores = (probs * (grad_probs - delta[h : h + 1, :])).astype(BF16)
            grad_values = grad_values + dot(probs.astype(BF16), grad_h)
            grad_keys = grad_keys + dot(grad_scores, query_h)
            grad_queries = grad_queries + jnp.where(mine, dot(grad_scores, keys, TN), 0.0)
        out_ref[low:high, :lanes] = (grad_queries * SCALE).astype(BF16)
        if b:
            dk_ref[:low, :] = dk_ref[:low, :] + grad_keys[:low, :]
            dv_ref[:low, :] = dv_ref[:low, :] + grad_values[:low, :]
        dk_ref[low:high, :] = grad_keys[low:, :]
        dv_ref[low:high, :] = grad_values[low:, :]
    out_ref[:, lanes : 2 * lanes] = dk_ref[...].astype(BF16)
    out_ref[:, 2 * lanes :] = dv_ref[...].astype(BF16)


def attention_forward(qkv, seg_col, seg_row, earlier):
    rows, lanes = qkv.shape[0], qkv.shape[1] // 3
    heads = lanes // HEAD_DIM
    pairs = rows * rows * heads // 2
    return pl.pallas_call(
        lambda *refs: forward_kernel(*refs, heads=heads, lanes=lanes, block=QUERY_BLOCK),
        out_shape=(jax.ShapeDtypeStruct((rows, lanes), BF16), jax.ShapeDtypeStruct((heads, rows), F32)),
        compiler_params=pltpu.CompilerParams(vmem_limit_bytes=48 * 2**20),
        cost_estimate=pl.CostEstimate(flops=pairs * 5000, bytes_accessed=8 * rows * lanes, transcendentals=pairs),
        in_specs=[pl.BlockSpec(memory_space=pltpu.VMEM)] * 3 + [ANYWHERE] * len(earlier),
        name="attention_forward",
    )(qkv, seg_col, seg_row, *earlier)


def attention_backward(qkv, grads, log_total, mixed, seg_col, seg_row, earlier):
    rows, lanes = qkv.shape[0], qkv.shape[1] // 3
    heads = lanes // HEAD_DIM
    pairs = rows * rows * heads // 2
    return pl.pallas_call(
        lambda *refs: backward_kernel(*refs, heads=heads, lanes=lanes, block=QUERY_BLOCK),
        out_shape=jax.ShapeDtypeStruct((rows, 3 * lanes), BF16),
        scratch_shapes=[pltpu.VMEM((rows, lanes), F32), pltpu.VMEM((rows, lanes), F32)],
        compiler_params=pltpu.CompilerParams(vmem_limit_bytes=48 * 2**20),
        cost_estimate=pl.CostEstimate(flops=pairs * 5000, bytes_accessed=14 * rows * lanes, transcendentals=pairs),
        in_specs=[pl.BlockSpec(memory_space=pltpu.VMEM)] * 6 + [ANYWHERE] * len(earlier),
        name="attention_backward",
    )(qkv, grads, log_total, mixed, seg_col, seg_row, *earlier)


def feed_kernel(normed_ref, grad_ref, up_ref, bias_ref, down_ref, hidden_ref, pre_ref, sum_ref):
    block = 2 * QUERY_BLOCK
    total = jnp.zeros(sum_ref.shape, F32)
    down = jnp.transpose(down_ref[...])
    for low in range(0, normed_ref.shape[0], block):
        rows = slice(low, low + block)
        u = dot(normed_ref[rows, :], up_ref[...]) + bias_ref[...]
        grad_hidden = dot(grad_ref[rows, :], down)
        square = u * u
        bend = jnp.tanh(u * (0.7978845608028654 + (0.7978845608028654 * 0.044715) * square))
        half = 0.5 + 0.5 * bend
        hidden_ref[rows, :] = (u * half).astype(BF16)
        slope = half + u * (half * (1.0 - bend)) * (
            0.7978845608028654 + (3.0 * 0.7978845608028654 * 0.044715) * square
        )
        grad_pre = (grad_hidden * slope).astype(BF16)
        pre_ref[rows, :] = grad_pre
        total = total + jnp.sum(grad_pre.astype(F32), axis=0, keepdims=True)
    sum_ref[...] = total


def feed_forward(normed, grad, w_up, bias, w_down):
    rows, width = normed.shape
    units = w_up.shape[1]
    tile = min(units, 256)
    whole = pl.BlockSpec((rows, width), lambda i: (0, 0))
    column = pl.BlockSpec((rows, tile), lambda i: (0, i))
    line = pl.BlockSpec((1, tile), lambda i: (0, i))
    return pl.pallas_call(
        feed_kernel,
        grid=(units // tile,),
        out_shape=(
            jax.ShapeDtypeStruct((rows, units), BF16),
            jax.ShapeDtypeStruct((rows, units), BF16),
            jax.ShapeDtypeStruct((1, units), F32),
        ),
        in_specs=[
            whole,
            whole,
            pl.BlockSpec((width, tile), lambda i: (0, i)),
            line,
            pl.BlockSpec((tile, width), lambda i: (i, 0)),
        ],
        out_specs=(column, column, line),
        compiler_params=pltpu.CompilerParams(vmem_limit_bytes=56 * 2**20),
        cost_estimate=pl.CostEstimate(
            flops=4 * rows * width * units, bytes_accessed=4 * rows * width, transcendentals=rows * units
        ),
        name="feed_forward",
    )(normed, grad, w_up, bias, w_down)


def chips():
    return lax.axis_size("ctx") // 2


def turn(value, k):
    count = chips()
    return lax.ppermute(
        value, "ctx", [(2 * s + core, 2 * ((s + k) % count) + core) for s in range(count) for core in range(2)]
    )


FAR = ((0, 2), (1, 3), (2, 0), (3, 1))
NEAR = ((0, 1), (1, 0), (2, 3), (3, 2))
MIDDLE = ((1, 2), (2, 1))
OUT = ((2, 3), (1, 0))
BACK = ((3, 2), (0, 1))


def chip_permute(value, pairs):
    return lax.ppermute(value, "ctx", [(2 * s + core, 2 * t + core) for s, t in pairs for core in range(2)])


def swap(value):
    return lax.ppermute(value, "ctx", [(i, i ^ 1) for i in range(2 * chips())])


def place():
    me = lax.axis_index("ctx")
    return me // 2, me % 2


def after(value, *earlier, cost=0):
    def nothing(*refs):
        pass

    return pl.pallas_call(
        nothing,
        out_shape=jax.ShapeDtypeStruct(value.shape, value.dtype),
        in_specs=[ANYWHERE] * (1 + len(earlier)),
        out_specs=ANYWHERE,
        input_output_aliases={0: 0},
        cost_estimate=pl.CostEstimate(flops=cost * 10**9, bytes_accessed=cost * 3 * 10**6, transcendentals=0),
        name="after",
    )(value, *earlier)


def gather_ctx(block, relay=False):
    count = chips()
    chip, core = place()
    if relay and count == 4:
        far, near, middle = (chip_permute(block, pairs) for pairs in (FAR, NEAR, MIDDLE))
        last = jnp.where((chip == 0) | (chip == 3), chip_permute(far, OUT), middle)
        same, chip_of = [block, near, far, last], [chip, chip ^ 1, chip ^ 2, chip ^ 3]
    else:
        same = [block] + [turn(block, k) for k in range(1, count)]
        chip_of = [(chip + count - k) % count for k in range(count)]
    other = [swap(item) for item in same]
    out = jnp.zeros((2 * count,) + block.shape, block.dtype)
    for k in range(count):
        base = 2 * chip_of[k]
        out = lax.dynamic_update_index_in_dim(out, same[k], base + core, 0)
        out = lax.dynamic_update_index_in_dim(out, other[k], base + 1 - core, 0)
    return out, same[1]


def where_am_i():
    return jnp.stack(place()).astype(jnp.int32)


def pack_columns(weights, cuts, vectors):
    count = chips()
    r = weights[0].shape[0]
    total = sum(lead * width for lead, width in cuts)
    below = -(-len(vectors) // 16) * 16

    def kernel(at_ref, *refs):
        ins, outs = refs[: len(weights)], refs[-(count + 1) :]
        chip, core = at_ref[0], at_ref[1]
        for j in range(2 * count):
            pieces = [
                ref[:, (a * 2 * count + j) * width : (a * 2 * count + j + 1) * width]
                for ref, (lead, width) in zip(ins, cuts)
                for a in range(lead)
            ]
            block = jnp.concatenate(pieces, axis=1)
            slot = lax.rem(j // 2 + count - chip, count)
            for k in range(count):

                @pl.when((slot == k) & (core == j % 2))
                def _(k=k, block=block):
                    outs[k][:r, :] = block

                @pl.when((slot == k) & (core != j % 2))
                def _(k=k, block=block):
                    outs[count][k, :r, :] = block

        if vectors:
            lines = [ref[...].astype(F32) for ref in refs[len(weights) : len(weights) + len(vectors)]]
            lines = [
                jnp.concatenate([line, jnp.zeros((1, total - line.shape[1]), F32)], axis=1) for line in lines
            ]
            more = jnp.concatenate(lines + [jnp.zeros((below - len(lines), total), F32)], axis=0).astype(BF16)
            for k in range(count):
                outs[k][r:, :] = more
                outs[count][k, r:, :] = more

    block_shape = jax.ShapeDtypeStruct((r + below, total), BF16)
    return pl.pallas_call(
        kernel,
        out_shape=[block_shape] * count + [jax.ShapeDtypeStruct((count,) + block_shape.shape, BF16)],
        in_specs=[pl.BlockSpec(memory_space=pltpu.SMEM)]
        + [pl.BlockSpec(memory_space=pltpu.VMEM)] * (len(weights) + len(vectors)),
        name="pack_columns",
    )(where_am_i(), *weights, *vectors)


def pack_rows(arrays, more, height):
    count = chips()
    width = sum(item.shape[1] for item in arrays)
    total = width + more.shape[2]

    def kernel(at_ref, *refs):
        ins, outs = refs[: len(arrays)], refs[-(count + 1) :]
        chip, core = at_ref[0], at_ref[1]
        for k in range(count):
            base = 2 * lax.rem(chip + k, count)
            start = 0
            for ref in ins:
                end = start + ref.shape[1]
                mine = pl.ds(pl.multiple_of((base + core) * height, height), height)
                other = pl.ds(pl.multiple_of((base + 1 - core) * height, height), height)
                outs[k][:, start:end] = ref[mine, :]
                outs[count][k, :, start:end] = ref[other, :]
                start = end
            outs[k][:, width:] = refs[len(arrays)][base + core]
            outs[count][k, :, width:] = refs[len(arrays)][base + 1 - core]

    block_shape = jax.ShapeDtypeStruct((height, total), BF16)
    return pl.pallas_call(
        kernel,
        out_shape=[block_shape] * count + [jax.ShapeDtypeStruct((count,) + block_shape.shape, BF16)],
        in_specs=[pl.BlockSpec(memory_space=pltpu.SMEM)] + [pl.BlockSpec(memory_space=pltpu.VMEM)] * (1 + len(arrays)),
        name="pack_rows",
    )(where_am_i(), *arrays, more)


def exchange_ctx(packed):
    count = chips()
    arrived = swap(packed[count])
    both = [jnp.stack([packed[k], arrived[k]]) for k in range(count)]
    return [both[0]] + [turn(both[k], k) for k in range(1, count)]


def source_index(at_ref, k, side, count):
    core = at_ref[1] if side == 0 else 1 - at_ref[1]
    return 2 * lax.rem(at_ref[0] + count - k, count) + core


def unpack_to_rows(got, r, widths, earlier):
    count = chips()
    height, total = got[0].shape[1:]
    below = height - r

    def kernel(at_ref, *refs):
        ins, outs = refs[:count], refs[count + len(earlier) :]
        for k in range(count):
            for side in range(2):
                index = source_index(at_ref, k, side, count)
                start = 0
                for out, width in zip(outs, widths):
                    out[pl.ds(pl.multiple_of(index * r, r), r), :] = ins[k][side, :r, start : start + width]
                    start += width
                if below:
                    outs[-1][index] = ins[k][side, r:, :]

    return pl.pallas_call(
        kernel,
        out_shape=[jax.ShapeDtypeStruct((2 * count * r, width), BF16) for width in widths]
        + [jax.ShapeDtypeStruct((2 * count, below, total), BF16)] * (below > 0),
        in_specs=[pl.BlockSpec(memory_space=pltpu.SMEM)]
        + [pl.BlockSpec(memory_space=pltpu.VMEM)] * count
        + [ANYWHERE] * len(earlier),
        name="unpack_to_rows",
    )(where_am_i(), *got, *earlier)


def unpack_to_columns(got, cuts, lengths):
    count = chips()
    r, total = got[0].shape[1:]

    def kernel(at_ref, *refs):
        ins, outs, held = refs[:count], refs[count:-1], refs[-1]
        for k in range(count):
            for side in range(2):
                held[source_index(at_ref, k, side, count)] = ins[k][side]
        for j in range(2 * count):
            block = held[j].astype(F32)
            start = 0
            for out, (lead, width) in zip(outs, cuts):
                for a in range(lead):
                    column = (a * 2 * count + j) * width
                    out[:, column : column + width] = block[:, start : start + width]
                    start += width
        added = held[0, :, total - 128 :].astype(F32)
        for j in range(1, 2 * count):
            added = added + held[j, :, total - 128 :].astype(F32)
        lines = jnp.transpose(added)
        columns = sum(lengths) // r
        at = 0
        for out, length in zip(outs[len(cuts) :], lengths):
            parts = [
                lines[i : i + 1, :] + lines[columns + i : columns + i + 1, :] for i in range(at, at + length // r)
            ]
            out[...] = parts[0] if len(parts) == 1 else jnp.concatenate(parts, axis=1)
            at += length // r

    return pl.pallas_call(
        kernel,
        out_shape=[jax.ShapeDtypeStruct((r, 2 * count * lead * width), F32) for lead, width in cuts]
        + [jax.ShapeDtypeStruct((1, length), F32) for length in lengths],
        in_specs=[pl.BlockSpec(memory_space=pltpu.SMEM)] + [pl.BlockSpec(memory_space=pltpu.VMEM)] * count,
        scratch_shapes=[pltpu.VMEM((2 * count, r, total), BF16)],
        name="unpack_to_columns",
    )(where_am_i(), *got)


def split_rows(rows, relay):
    count = chips()
    chip, core = place()
    pairs = rows.reshape((count, 2, rows.shape[0] // (2 * count), rows.shape[1]))
    order = [chip ^ (3 - k) for k in range(4)] if relay and count == 4 else [(chip + k) % count for k in range(1, count + 1)]
    turned = [lax.dynamic_index_in_dim(pairs, index, 0, keepdims=False) for index in order]
    pick = lambda which: jnp.concatenate(
        [lax.dynamic_index_in_dim(item, which, 0, keepdims=False) for item in turned], axis=0
    )
    return pick(core), pick(1 - core)


def chip_sums(left, right, dims, earlier=(), relay=False):
    count = chips()
    mine, other = split_rows(left, relay)
    leaving = dot(other, right, dims).astype(BF16)
    arrived = swap(after(leaving, *earlier) if earlier else leaving)
    own = dot(mine, right, dims)
    n = own.shape[0] // count
    sums = [own[k * n : (k + 1) * n] + arrived[k * n : (k + 1) * n].astype(F32) for k in range(count)]
    return [item.astype(BF16) for item in sums[:-1]] + sums[-1:]


def add_over_chips(sums, earlier=(), relay=False):
    count = chips()
    total = sums[-1]
    if relay and count == 4:
        ends, middle, near = (chip_permute(*pair) for pair in ((sums[0], BACK), (sums[0], MIDDLE), (sums[2], NEAR)))
        far = chip_permute((sums[1].astype(F32) + ends.astype(F32)).astype(BF16), FAR)
        for arrived in (middle, near, far):
            arrived = after(arrived, *earlier) if earlier else arrived
            total = total + arrived.astype(F32)
        return total, near
    for k in range(1, count):
        arrived = turn(sums[k - 1], k)
        arrived = after(arrived, *earlier) if earlier else arrived
        total = total + arrived.astype(F32)
        first = arrived if k == 1 else first
    return total, first


def reduce_dp_small(blocks):
    parts = lax.axis_size("dp")
    me = lax.axis_index("dp")
    total = lax.dynamic_index_in_dim(blocks, me, 0, keepdims=False)
    for k in range(1, parts):
        piece = lax.dynamic_index_in_dim(blocks, (me + k) % parts, 0, keepdims=False)
        total = total + lax.ppermute(piece, "dp", [(i, (i + k) % parts) for i in range(parts)])
    return total


def gather_dp(value):
    return lax.all_gather(value, "dp", axis=0, tiled=True)


def scatter_dp(value):
    return lax.psum_scatter(value, "dp", scatter_dimension=0, tiled=True)


def across(value, k):
    return lax.ppermute(value, "dp", [(i, i ^ k) for i in range(lax.axis_size("dp"))])


def turn_gather_dp(value):
    parts = lax.axis_size("dp")
    me = lax.axis_index("dp")
    out = jnp.zeros((parts,) + value.shape, value.dtype)
    out = lax.dynamic_update_index_in_dim(out, value, me, 0)
    for k in range(1, parts):
        out = lax.dynamic_update_index_in_dim(out, across(value, k), me ^ k, 0)
    return out.reshape((parts * value.shape[0],) + value.shape[1:])


def turn_scatter_dp(blocks):
    parts = lax.axis_size("dp")
    me = lax.axis_index("dp")
    blocks = blocks.reshape((parts, blocks.shape[0] // parts) + blocks.shape[1:])
    total = lax.dynamic_index_in_dim(blocks, me, 0, keepdims=False).astype(F32)
    for k in range(1, parts):
        total = total + across(lax.dynamic_index_in_dim(blocks, me ^ k, 0, keepdims=False), k).astype(F32)
    return total


def standardize(values):
    average = jnp.mean(values, axis=-1, keepdims=True)
    centered = values - average
    variance = jnp.mean(centered * centered, axis=-1, keepdims=True)
    factor = lax.rsqrt(variance + EPSILON)
    return centered * factor, factor


def norm_back(grad, gain, standard, factor):
    scaled = grad * gain
    return (
        scaled
        - jnp.mean(scaled, axis=-1, keepdims=True)
        - standard * jnp.mean(scaled * standard, axis=-1, keepdims=True)
    ) * factor


def local(
    tokens_in,
    exit_layer,
    layer_index,
    segment_ids,
    grad_out,
    first_gain,
    first_bias,
    query_weight,
    query_bias,
    key_weight,
    value_weight,
    value_bias,
    out_weight,
    out_bias,
    second_gain,
    second_bias,
    up_weight,
    up_bias,
    down_weight,
    down_bias,
):
    T, N = lax.axis_size("ctx"), lax.axis_size("dp")
    me = lax.axis_index("ctx")
    n, D = tokens_in.shape[1], tokens_in.shape[2]
    r = first_gain.shape[0]
    f = up_bias.shape[0]
    S = T * n
    B = max(HEAD_DIM, r)
    A = D // (T * B)
    L = A * B
    x = tokens_in[0]
    g_out = grad_out[0]
    active = (exit_layer[0] > layer_index[0]).astype(F32)

    x_all = lax.all_gather(x, "ctx", axis=0, tiled=True)
    natural = r % HEAD_DIM == 0
    if natural:
        w_out = turn_gather_dp(out_weight)
    else:
        w_all = lax.all_gather(out_weight, ("dp", "ctx"), axis=0, tiled=True).reshape(A, T, B, D)
        w_out = lax.dynamic_index_in_dim(w_all, me, 1, keepdims=False).reshape(L, D)
    vectors = [first_gain, first_bias, query_bias, value_bias, out_bias, second_gain, second_bias, down_bias, up_bias]
    vectors = [v.reshape(1, -1) for v in vectors + [active.astype(BF16), segment_ids[0].astype(BF16)]]
    got = exchange_ctx(pack_columns([query_weight, key_weight, value_weight], [(A, B)] * 3, vectors))
    qkv_rows, small_got = unpack_to_rows(got, r, (3 * L,), (x_all, w_out))
    up_packed = pack_columns([up_weight], [(N, f)], [])
    w_qkv = gather_dp(qkv_rows)
    small_width = max(r, f)
    params = turn_gather_dp(small_got[:, :9, :small_width].reshape(T * 9, small_width)).reshape(N, T, 9, small_width)
    g_all, g_begun = gather_ctx(after(g_out, qkv_rows))
    g_all = g_all.reshape(S, D)

    feature = lambda i: params[:, :, i, :r].reshape(D).astype(F32)
    gain_one, bias_one, bias_query, bias_value, bias_out, gain_two, bias_two, bias_down = (
        feature(i) for i in range(8)
    )
    bias_up = lax.dynamic_index_in_dim(params[:, :, 8, :f], me, 1, keepdims=False).reshape(N * f).astype(F32)
    active_row = small_got[:, 9, :n].reshape(S)
    segs = small_got[:, 10, :n].reshape(S).astype(jnp.int32)
    seg_col, seg_row = segs.reshape(S, 1), segs.reshape(1, S)
    own_heads = lambda v: lax.dynamic_index_in_dim(v.reshape(A, T, B), me, 1, keepdims=False).reshape(L)
    bias_qkv = jnp.concatenate([own_heads(bias_query), jnp.zeros((L,), F32), own_heads(bias_value)])

    standard_one, _ = standardize(x_all.astype(F32))
    normed_one = after((standard_one * gain_one + bias_one).astype(BF16), g_all)
    qkv = (dot(normed_one, w_qkv) + bias_qkv).astype(BF16)
    w_down = gather_dp(after(down_weight, qkv))
    up_got = exchange_ctx([*up_packed[:-1], after(up_packed[-1], g_begun)])
    mixed, log_total = attention_forward(qkv, seg_col, seg_row, ())
    (up_rows,) = unpack_to_rows(up_got, r, (N * f,), (mixed,))
    w_up = gather_dp(up_rows)
    branch = add_over_chips(chip_sums(mixed, w_out, NN, (up_rows,), True), relay=True)[0] + bias_out
    inputs = x.astype(F32)
    active_own = active[:, None]
    middle = inputs + active_own * branch

    standard_two, factor_two = standardize(middle)
    normed_two = (standard_two * gain_two + bias_two).astype(BF16)
    normed_two_all = gather_ctx(after(normed_two, cost=0), True)[0].reshape(S, D)
    grad_ffn = (active_row[:, None] * g_all).astype(BF16)
    hidden, grad_pre, grad_up_sum = feed_forward(normed_two_all, grad_ffn, w_up, bias_up.reshape(1, N * f), w_down)
    sums_two = chip_sums(grad_pre, w_up, NT)
    grad_normed_two, begun_two = add_over_chips(sums_two)
    hidden = after(hidden, sums_two[0])
    grad_down_part = dot(hidden, grad_ffn, TN).astype(BF16)
    grad_down = scatter_dp(grad_down_part)
    grad_up_part = dot(after(normed_two_all, sums_two[0]), grad_pre, TN).astype(BF16)
    grad_up_mine = scatter_dp(grad_up_part)
    feed_sums = chip_sums(after(hidden, begun_two), w_down, NN, relay=True)
    grad_res = g_out.astype(F32)
    grad_middle = grad_res + norm_back(grad_normed_two, gain_two, standard_two, factor_two)
    grad_branch = after((active_own * grad_middle).astype(BF16), cost=250)

    grad_branch_all = gather_ctx(grad_branch)[0].reshape(S, D)
    grad_heads = dot(grad_branch_all, w_out, NT).astype(BF16)
    grad_out_w = dot(mixed, grad_branch_all, TN)
    if natural:
        grad_out_w = scatter_dp(grad_out_w.astype(BF16))
    else:
        spread = jnp.zeros((A, T, B, D), F32)
        spread = lax.dynamic_update_index_in_dim(spread, grad_out_w.reshape(A, B, D), me, 1)
        grad_out_w = lax.psum_scatter(spread.reshape(D, D), ("dp", "ctx"), scatter_dimension=0, tiled=True)
    grad_qkv = attention_backward(
        qkv, grad_heads, log_total, mixed, seg_col, seg_row, (grad_down, grad_up_mine)
    )

    grad_qkv_part = dot(normed_one, grad_qkv, TN).astype(BF16)
    feed, _ = add_over_chips([after(item, grad_branch_all) for item in feed_sums[:-1]] + feed_sums[-1:], (grad_qkv,), True)
    sums_one = chip_sums(grad_qkv, w_qkv, NT, (grad_qkv_part, feed, grad_out_w))
    grad_normed_one, begun_one = add_over_chips(sums_one)
    grad_normed_one = after(grad_normed_one, cost=0)
    layer_out = (middle + active_own * (feed + bias_down)).astype(BF16)[None]
    standard_in, factor_in = standardize(inputs)
    grad_in = (grad_middle + norm_back(grad_normed_one, gain_one, standard_in, factor_in)).astype(BF16)[None]

    partial_one = dot(after(grad_qkv, begun_one), w_qkv, NT)
    grad_gain_one = jnp.sum(partial_one * standard_one, axis=0)
    grad_bias_one = jnp.sum(partial_one, axis=0)
    grad_gain_two = jnp.sum(grad_normed_two * standard_two, axis=0)
    grad_bias_two = jnp.sum(grad_normed_two, axis=0)
    ctx_index = lax.broadcasted_iota(jnp.int32, (1, T, 1), 1)
    spread_heads = lambda v: jnp.where(ctx_index == me, v.reshape(A, 1, B), 0.0).reshape(D)
    grad_bias_qkv = jnp.sum(grad_qkv.astype(F32), axis=0)
    grad_out_sum = jnp.sum(grad_branch.astype(F32), axis=0)
    grad_down_sum = jnp.sum((active_own * grad_res), axis=0)
    features = jnp.stack(
        [
            grad_gain_one,
            grad_bias_one,
            spread_heads(grad_bias_qkv[:L]),
            spread_heads(grad_bias_qkv[2 * L :]),
            grad_out_sum,
            grad_gain_two,
            grad_bias_two,
            grad_down_sum,
        ]
    )
    features = features.reshape(8, N, T, r).transpose(1, 2, 0, 3).reshape(N, T, 8 * r)
    units = jnp.where(
        lax.broadcasted_iota(jnp.int32, (1, T, 1), 1) == me, grad_up_sum.reshape(N, 1, f), 0.0
    )
    sums = jnp.concatenate([features, units], axis=2).reshape(N, T * (8 * r + f))
    sums = reduce_dp_small(sums).reshape(T, 8 * r + f)
    grad_qkv_mine = scatter_dp(grad_qkv_part)
    sums = sums.reshape(T, 8 + f // r, r).transpose(0, 2, 1)
    coarse = sums.astype(BF16)
    fine = (sums - coarse.astype(F32)).astype(BF16)
    more = jnp.pad(jnp.concatenate([coarse, fine], axis=2), ((0, 0), (0, 0), (0, 128 - 2 * sums.shape[2])))
    grad_got = exchange_ctx(pack_rows([after(grad_qkv_mine, grad_normed_one), grad_up_mine], more, r))
    grad_q, grad_k, grad_v, grad_up, *lines = unpack_to_columns(grad_got, [(A, B)] * 3 + [(N, f)], [r] * 8 + [f])
    shard = lambda i: lines[i].reshape(-1)
    return (
        layer_out,
        grad_in,
        shard(0),
        shard(1),
        grad_q,
        shard(2),
        grad_k,
        grad_v,
        shard(3),
        grad_out_w.astype(F32),
        shard(4),
        shard(5),
        shard(6),
        grad_up,
        shard(8),
        after(grad_down, grad_got[0]).astype(F32),
        shard(7),
    )


def solution(mesh):
    rows = P("dp", "ctx", None)
    flags = P("dp", "ctx")
    vector = P(("dp", "ctx"))
    matrix = P(("dp", "ctx"), None)
    in_specs = (
        rows, flags, P(), flags, rows, vector, vector, matrix, vector, matrix,
        matrix, vector, matrix, vector, vector, vector, matrix, vector, matrix, vector,
    )
    out_specs = (
        rows, rows, vector, vector, matrix, vector, matrix, matrix, vector, matrix,
        vector, vector, vector, matrix, vector, matrix, vector,
    )
    return jax.shard_map(local, mesh=mesh, in_specs=in_specs, out_specs=out_specs, check_vma=False)
```
